32 devices in a mesh: tm: 4 (over y, x), lat: 8 (over z, core).
Axes of the slice: x: 2, y: 2, z: 4, core: 2. Of those that a mesh axis runs over, the one named last changes fastest.
Arguments:
- cotangent: float32 [16, 128, 2048], P('tm', 'lat'), may hold values from -6 to 6
- iterates: float32 [3, 16, 128, 2048], P(None, 'tm', 'lat'), may hold values from -6 to 6
- range_field: float32 [128, 2048], P('lat', 'tm'), may hold values from 0.05 to 1
Outputs:
- noise_cotangent: float32 [16, 128, 2048], P('tm', 'lat')
- range_gradient: float32 [128, 2048], P('lat', 'tm')
The draws below stay inside these ranges and needn't reach their ends.
All inputs are finite; a program needn't handle non-finite values.
Results may differ from the reference program's by a relative error of at most 0.0001.
Values sent between devices are 32-bit elements; how exact they have to be, the bound alone decides.
No kernel may reach another device: no remote copies, remote signals or barrier semaphores. Data moves between devices by JAX's collectives and lax.ppermute only.
A program may use at most 64 MiB of HBM per device.

```python
import math
import jax
import jax.numpy as jnp

NX = 2048
STEPS = 4
TIMES = 16
NY = 128


def steps_of(key, dims, cuts, low, high):
    factor_of = 1.0
    for axis_at, blocks in cuts:
        draws = jax.random.uniform(jax.random.fold_in(jax.random.fold_in(key, 6), axis_at), (blocks,), jnp.float32, low / len(cuts), high / len(cuts))
        factor_of = factor_of * jnp.repeat(jnp.exp(draws), dims[axis_at] // blocks).reshape((-1,) + (1,) * (len(dims) - 1 - axis_at))
    return factor_of


def scatter_about(key, shape, spread, most, shards=(), kind=jnp.bfloat16):
    array = jax.random.normal(key, shape, jnp.float32) * spread
    if len(shards) > 0:
        array = steps_of(key, shape, shards, -0.22, 0.18) * array
    return jnp.clip(array, min=-most, max=most).astype(kind)


def setup_inputs(seed: int = 0) -> dict:
    arg_keys = jax.random.split(jax.random.key(seed), 4)
    cotangent = scatter_about(arg_keys[0], (TIMES, NY, NX), 1.0, 6.0, ((0, 4), (1, 8)), jnp.float32)
    iterates = scatter_about(arg_keys[1], (STEPS - 1, TIMES, NY, NX), 1.0, 6.0, ((1, 4), (2, 8)), jnp.float32)
    range_field = jnp.clip(jnp.exp(math.log(1.0) - 2.9957323 * jax.random.uniform(arg_keys[2], (NY, NX), jnp.float32) ** steps_of(arg_keys[2], (NY, NX), ((0, 8), (1, 4)), -0.2, 0.2)), 0.05, 1.0)
    return {"cotangent": cotangent, "iterates": iterates, "range_field": range_field}


def step_weights():
    centre_value = 6.525
    spread_value = 6.475
    root_order = (3, 0, 2, 1)
    return [1.0 / (centre_value + spread_value * math.cos(math.pi * (2 * section + 1) / 8.0)) for section in root_order]


def operate(field, coefficient):
    padded = jnp.pad(field, ((1, 1), (1, 1), (0, 0)))
    latitude = padded[1:-1, 2:, :] + padded[1:-1, :-2, :]
    longitude = jnp.roll(field, 1, 2) + jnp.roll(field, -1, 2)
    temporal = padded[2:, 1:-1, :] + padded[:-2, 1:-1, :]
    return (coefficient[None, :, :] + 6.0) * field - latitude - longitude - temporal


def reference(cotangent, iterates, range_field):
    weights = step_weights()
    adjoint = cotangent
    noise_cot = weights[3] * cotangent
    gradient = jnp.zeros(range_field.shape, jnp.float32)
    for section in (3, 2, 1):
        gradient = gradient - weights[section] * jnp.sum(adjoint * iterates[section - 1], axis=0)
        adjoint = adjoint - weights[section] * operate(adjoint, range_field)
        noise_cot = noise_cot + weights[section - 1] * adjoint
    return noise_cot, gradient
```

```python
import functools
import math

import jax
import jax.numpy as jnp
from jax import lax
from jax.experimental import pallas as pl
from jax.experimental.pallas import tpu as pltpu
from jax.sharding import PartitionSpec as P

F32 = jnp.float32
LANES = 128
SLICES = 4
HELD = 24


def step_weights():
    centre_value = 6.525
    spread_value = 6.475
    root_order = (3, 0, 2, 1)
    return [
        1.0 / (centre_value + spread_value * math.cos(math.pi * (2 * section + 1) / 8.0))
        for section in root_order
    ]


W0, W1, W2, W3 = step_weights()


def even_pairs(count):
    return [(i, i ^ 1) for i in range(count)]


def odd_pairs(count):
    return [(i, (i + 1) % count if i % 2 else (i - 1) % count) for i in range(count)]


def shape_of(*dims):
    return jax.ShapeDtypeStruct(dims, F32)


def call(kernel, outs, *args, scratch=()):
    spec = pl.BlockSpec(memory_space=pltpu.VMEM)
    many = isinstance(outs, (list, tuple))
    return pl.pallas_call(
        kernel,
        out_shape=outs,
        in_specs=[spec] * len(args),
        out_specs=[spec] * len(outs) if many else spec,
        scratch_shapes=scratch,
        compiler_params=pltpu.CompilerParams(vmem_limit_bytes=12 << 20),
    )(*args)


def each_tile(width, work):
    def step(tile, carry):
        work(tile, pl.ds(pl.multiple_of(tile * LANES, LANES), LANES))
        return carry

    lax.fori_loop(0, width // LANES, step, 0)


def iota(rows, dim):
    return lax.broadcasted_iota(jnp.int32, (rows, LANES), dim)


def down(cells, by):
    return pltpu.roll(cells, by, 0)


def around(ref, index, tile, tiles):
    def cols(at):
        return pl.ds(pl.multiple_of(at * LANES, LANES), LANES)

    cells = ref[index, :, cols(tile)]
    before = ref[index, :, cols(lax.rem(tile + tiles - 1, tiles))]
    after = ref[index, :, cols(lax.rem(tile + 1, tiles))]
    lane = iota(HELD, 1)
    west = pltpu.roll(jnp.where(lane == LANES - 1, before, cells), 1, 1)
    east = pltpu.roll(jnp.where(lane == 0, after, cells), LANES - 1, 1)
    return cells, west + east + (down(cells, 1) + down(cells, HELD - 1))


def places(tm_count):
    t = lax.axis_index("tm")
    odd = lax.rem(t, 2)
    open_side = jnp.where(odd == 1, t < tm_count - 1, t > 0).astype(F32)
    return t, odd, open_side


def mirrored(odd, j):
    return jnp.where(odd == 1, SLICES - 1 - j, j)


def lat_mask(lat_count):
    l = lax.axis_index("lat")
    row = iota(HELD, 0)
    below = (l < lat_count - 1).astype(F32)
    above = (l > 0).astype(F32)
    return jnp.where(row < HELD - 8, 1.0, jnp.where(row < HELD - 4, below, above))


def first_kernel(forward, cot, rng, own, e1, o1, e2, o2):
    _, odd, _ = places(2)
    rows, width = cot.shape[1:]
    chunk = rng.shape[1]
    blocks = width // chunk
    for j in range(SLICES):
        own[j] = cot[pl.ds(mirrored(odd, j), 1)][0]
    for out, j in ((e1, SLICES - 1), (o1, 0)):
        for b in range(blocks):
            out[b * rows : (b + 1) * rows] = own[j, :, b * chunk : (b + 1) * chunk]
        out[blocks * rows :] = rng[...]
    for out, js in ((e2, (SLICES - 2, SLICES - 3)), (o2, (1, 2))):
        for i, j in enumerate(js[: 1 if forward else 2]):
            out[i * rows : (i + 1) * rows] = own[j]


def slab(ref, tile, rows, chunk):
    per = chunk // LANES
    at = pl.multiple_of(lax.div(tile, per) * rows, rows)
    cols = pl.ds(pl.multiple_of(lax.rem(tile, per) * LANES, LANES), LANES)
    return ref[pl.ds(at, rows), cols]


def rows_kernel(forward, own, e1, o1, *refs):
    rows, width = own.shape[1:]
    chunk = e1.shape[1]
    blocks = width // chunk
    if forward:
        rng, far, la, lb, full = refs
        t, _, _ = places(2)
        for piece, owner in (
            (rng[...], t),
            (e1[blocks * rows :], t ^ 1),
            (far[...], t ^ 2),
            (o1[blocks * rows :], t ^ 3),
        ):
            full[:, pl.ds(pl.multiple_of(owner * chunk, chunk), chunk)] = piece
    else:
        gathered, la, lb, full = refs
        full[...] = gathered[...]
    even = lax.rem(lax.axis_index("lat"), 2) == 0
    sub = iota(8, 0)

    def work(tile, cols):
        cells = [own[j, :, cols] for j in range(SLICES)]
        near_e = slab(e1, tile, rows, chunk)
        near_o = slab(o1, tile, rows, chunk)
        field = full[:, cols]

        def low(x):
            return x[:8]

        def high(x):
            return x[rows - 8 :]

        first = (
            jnp.where(sub < 4, low(cells[0]), down(low(cells[1]), 5)),
            jnp.where(sub < 4, low(cells[2]), down(low(cells[3]), 5)),
            jnp.where(sub < 2, low(near_e), jnp.where(sub < 4, down(low(near_o), 2), down(low(field), 4))),
        )
        last = (
            jnp.where(sub >= 4, high(cells[0]), down(high(cells[1]), 3)),
            jnp.where(sub >= 4, high(cells[2]), down(high(cells[3]), 3)),
            jnp.where(sub >= 6, high(near_e), jnp.where(sub >= 4, down(high(near_o), 6), down(high(field), 4))),
        )
        for i in range(3):
            la[i * 8 : i * 8 + 8, cols] = jnp.where(even, last[i], first[i])
            lb[i * 8 : i * 8 + 8, cols] = jnp.where(even, first[i], last[i])

    each_tile(width, work)


def main_kernel(counts, own, e1, o1, full, la, lb, its, u, a3, q, part, grad, rr):
    tm_count, lat_count = counts
    _, odd, open_side = places(tm_count)
    rows, width = own.shape[1:]
    chunk = e1.shape[1]
    tiles = width // LANES
    mask = lat_mask(lat_count)
    even = lax.rem(lax.axis_index("lat"), 2) == 0
    sub = iota(8, 0)

    def gather(tile, cols):
        def joined(body, below, above):
            edge = jnp.where(sub < 4, below, above) * mask[rows:]
            return jnp.concatenate([body, edge], axis=0)

        below = [jnp.where(even, la[i : i + 8, cols], lb[i : i + 8, cols]) for i in (0, 8, 16)]
        above = [jnp.where(even, lb[i : i + 8, cols], la[i : i + 8, cols]) for i in (0, 8, 16)]
        for i in range(2):
            u[1 + 2 * i, :, cols] = joined(own[2 * i, :, cols], below[i], above[i])
            u[2 + 2 * i, :, cols] = joined(own[2 * i + 1, :, cols], down(below[i], 3), down(above[i], 5))
        near_o = joined(slab(o1, tile, rows, chunk), down(below[2], 6), down(above[2], 2))
        u[0, :, cols] = near_o * open_side
        u[SLICES + 1, :, cols] = joined(slab(e1, tile, rows, chunk), below[2], above[2])
        edge = jnp.where(sub < 4, down(below[2], 4), down(above[2], 4))
        rr[:, cols] = jnp.concatenate([full[:, cols], edge], axis=0) + 6.0

    each_tile(width, gather)

    def third(tile, cols):
        keep = (1.0 - W3 * rr[:, cols]) * mask
        pull = W3 * mask
        cells, sums = [], []
        for i in range(SLICES + 2):
            c, s = around(u, i, tile, tiles)
            cells.append(c)
            sums.append(s)
        for i in range(SLICES + 2):
            s = sums[i]
            if i > 0:
                s = s + cells[i - 1]
            if i < SLICES + 1:
                s = s + cells[i + 1]
            out = keep * cells[i] + pull * s
            a3[i, :, cols] = out * open_side if i == 0 else out

    each_tile(width, third)

    def second(tile, cols):
        keep = (1.0 - W2 * rr[:, cols]) * mask
        pull = W2 * mask
        cells = [a3[i, :, cols] for i in range(SLICES + 2)]
        total = jnp.zeros((rows, LANES), F32)
        for j in range(SLICES):
            c, s = around(a3, j + 1, tile, tiles)
            out = keep * c + pull * (s + cells[j] + cells[j + 2])
            q[j, :, cols] = out
            at = mirrored(odd, j)
            now, mid, start = out[:rows], c[:rows], u[j + 1, :rows, cols]
            part[j, :, cols] = W1 * now + W2 * mid + W3 * start
            x1, x2, x3 = (its[k, pl.ds(at, 1), :, cols][0] for k in range(3))
            total = total - (W3 * start * x3 + W2 * mid * x2 + W1 * now * x1)
        grad[:, cols] = total

    each_tile(width, second)


def late_kernel(tm_count, forward, grad, e2, o2, its, *refs):
    _, odd, open_side = places(tm_count)
    rows, width = grad.shape
    if forward:
        mine, g1, g2, g3, passed, total = refs
    else:
        (total,) = refs
    scale = -W1 * W2 * W3

    def work(tile, cols):
        x_o = its[0, pl.ds(mirrored(odd, 0), 1), :, cols][0]
        x_e = its[0, pl.ds(mirrored(odd, SLICES - 1), 1), :, cols][0]
        far_e, far_o = e2[:rows, cols], o2[:rows, cols]
        total[:, cols] = grad[:, cols] + scale * (far_e * x_e + far_o * open_side * x_o)
        if forward:
            passed[0, :, cols] = far_e
            passed[1, :, cols] = far_o

    each_tile(width, work)
    if forward:
        t = lax.axis_index("tm")
        chunk = mine.shape[1]
        for out, owner in ((mine, t), (g1, t ^ 1), (g2, t ^ 2), (g3, t ^ 3)):
            out[...] = total[:, pl.ds(pl.multiple_of(owner * chunk, chunk), chunk)]


def corner_kernel(e2, o2, la, lb):
    rows = 16
    width = la.shape[1]
    even = lax.rem(lax.axis_index("lat"), 2) == 0
    sub = iota(8, 0)

    def work(tile, cols):
        far_e, far_o = e2[:rows, cols], o2[:rows, cols]
        first = jnp.where(sub < 1, far_e[:8], down(far_o[:8], 1))
        last = jnp.where(sub >= 7, far_e[rows - 8 :], down(far_o[rows - 8 :], 7))
        la[:, cols] = jnp.where(even, last, first)
        lb[:, cols] = jnp.where(even, first, last)

    each_tile(width, work)


def last_kernel(counts, forward, u, a3, q, part, rr, e2, o2, *refs):
    tm_count, lat_count = counts
    if forward:
        passed, la, lb, noise, far, near, edge = refs
    else:
        la, lb, noise, far, near, edge = refs
    _, odd, open_side = places(tm_count)
    rows, width = part.shape[1:]
    tiles = width // LANES
    mask = lat_mask(lat_count)
    even = lax.rem(lax.axis_index("lat"), 2) == 0
    sub = iota(8, 0)

    def gather(tile, cols):
        below = jnp.where(even, la[:, cols], lb[:, cols])
        above = jnp.where(even, lb[:, cols], la[:, cols])

        def joined(body, below, above):
            return jnp.concatenate([body, jnp.where(sub < 4, below, above) * mask[rows:]], axis=0)

        far_o = joined(o2[:rows, cols], down(below, 7), down(above, 1)) * open_side
        far_e = joined(e2[:rows, cols], below, above)
        for i, cells, near_at, edge_at in ((0, far_o, 0, 0), (1, far_e, SLICES + 1, SLICES - 1)):
            far[i, :, cols] = cells
            near[i, :, cols] = a3[near_at, :, cols] + W3 * cells
            edge[i, :, cols] = q[edge_at, :, cols] + (W2 * W3) * cells

    each_tile(width, gather)

    def work(tile, cols):
        field = rr[:, cols]
        beyond = []
        for i in range(2):
            if forward:
                ends = passed[i, :, cols]
            else:
                ends = (o2, e2)[i][rows : 2 * rows, cols]
            c, s = around(far, i, tile, tiles)
            s = s[:rows] + u[(SLICES + 1) * i, :rows, cols] + ends
            third = (1.0 - W3 * field[:rows]) * c[:rows] + W3 * s
            c, s = around(near, i, tile, tiles)
            s = s[:rows] + third + a3[1 + (SLICES - 1) * i, :rows, cols]
            second = (1.0 - W2 * field[:rows]) * c[:rows] + W2 * s
            beyond.append(second * open_side if i == 0 else second)
        keep = 1.0 - W1 * field[:rows]
        cells, sums = [], []
        for j in range(SLICES):
            if j in (0, SLICES - 1):
                c, s = around(edge, min(j, 1), tile, tiles)
            else:
                c, s = around(q, j, tile, tiles)
            cells.append(c[:rows])
            sums.append(s[:rows])
        cells = [beyond[0], *cells, beyond[1]]
        for j in range(SLICES):
            s = sums[j] + cells[j] + cells[j + 2]
            first = keep * cells[j + 1] + W1 * s
            out = part[j, :, cols] + W0 * first
            if j in (0, SLICES - 1):
                out = out + (W1 * W2 * W3) * far[min(j, 1), :rows, cols]
            noise[pl.ds(mirrored(odd, j), 1), :, cols] = out[None]

    each_tile(width, work)


def body(counts, cotangent, iterates, range_field):
    tm_count, lat_count = counts
    forward = tm_count == 4
    slices, rows, width = cotangent.shape
    chunk = range_field.shape[1]
    assert slices == SLICES and rows == HELD - 8
    even, odd = even_pairs(tm_count), odd_pairs(tm_count)
    lat_even, lat_odd = even_pairs(lat_count), odd_pairs(lat_count)
    y_pairs = [(i, i ^ 2) for i in range(tm_count)]

    message = (width // chunk + 1) * rows
    deep = rows if forward else 2 * rows
    own, e1, o1, e2, o2 = call(
        functools.partial(first_kernel, forward),
        [shape_of(slices, rows, width)]
        + [shape_of(message, chunk)] * 2
        + [shape_of(deep, width)] * 2,
        cotangent,
        range_field,
    )
    e1 = lax.ppermute(e1, "tm", even)
    o1 = lax.ppermute(o1, "tm", odd)
    if forward:
        field = (range_field, lax.ppermute(range_field, "tm", y_pairs))
    else:
        field = (lax.all_gather(range_field, "tm", axis=1, tiled=True),)
    e2 = lax.ppermute(e2, "tm", even)
    o2 = lax.ppermute(o2, "tm", odd)

    la, lb, full = call(
        functools.partial(rows_kernel, forward),
        [shape_of(24, width)] * 2 + [shape_of(rows, width)],
        own,
        e1,
        o1,
        *field,
    )
    la = lax.ppermute(la, "lat", lat_even)
    lb = lax.ppermute(lb, "lat", lat_odd)

    held = shape_of(SLICES + 2, HELD, width)
    u, a3, q, part, grad, rr = call(
        functools.partial(main_kernel, counts),
        [
            held,
            held,
            shape_of(SLICES, HELD, width),
            shape_of(SLICES, rows, width),
            shape_of(rows, width),
            shape_of(HELD, width),
        ],
        own,
        e1,
        o1,
        full,
        la,
        lb,
        iterates,
    )
    if forward:
        mine, g1, g2, g3, passed = call(
            functools.partial(late_kernel, tm_count, True),
            [shape_of(rows, chunk)] * 4 + [shape_of(2, rows, width)],
            grad,
            e2,
            o2,
            iterates,
            scratch=[pltpu.VMEM((rows, width), F32)],
        )
        g1 = lax.ppermute(g1, "tm", even)
        g2 = lax.ppermute(g2, "tm", y_pairs)
        g3 = lax.ppermute(g3, "tm", odd)
        gradient = (mine + g1) + (g2 + g3)
        extra = (lax.ppermute(passed, "tm", y_pairs),)
    else:
        total = call(
            functools.partial(late_kernel, tm_count, False),
            shape_of(rows, width),
            grad,
            e2,
            o2,
            iterates,
        )
        gradient = lax.psum_scatter(total, "tm", scatter_dimension=1, tiled=True)
        extra = ()
    la, lb = call(corner_kernel, [shape_of(8, width)] * 2, e2, o2)
    la = lax.ppermute(la, "lat", lat_even)
    lb = lax.ppermute(lb, "lat", lat_odd)
    noise = call(
        functools.partial(last_kernel, counts, forward),
        shape_of(SLICES, rows, width),
        u,
        a3,
        q,
        part,
        rr,
        e2,
        o2,
        *extra,
        la,
        lb,
        scratch=[pltpu.VMEM((2, HELD, width), F32)] * 3,
    )
    return noise, gradient


def solution(mesh):
    counts = (mesh.shape["tm"], mesh.shape["lat"])
    return jax.shard_map(
        functools.partial(body, counts),
        mesh=mesh,
        in_specs=(P("tm", "lat", None), P(None, "tm", "lat", None), P("lat", "tm")),
        out_specs=(P("tm", "lat", None), P("lat", "tm")),
        check_vma=False,
    )
```

```python
import functools
import math

import jax
import jax.numpy as jnp
from jax import lax
from jax.experimental import pallas as pl
from jax.experimental.pallas import tpu as pltpu
from jax.sharding import PartitionSpec as P

F32 = jnp.float32
LANES = 128
SLICES = 4
ROWS = 16
HELD = 24


def step_weights():
    centre_value = 6.525
    spread_value = 6.475
    root_order = (3, 0, 2, 1)
    return [
        1.0 / (centre_value + spread_value * math.cos(math.pi * (2 * section + 1) / 8.0))
        for section in root_order
    ]


W0, W1, W2, W3 = step_weights()
SUM2 = W2 + W3
PROD2 = W2 * W3
COEFFS = (
    W0 + W1 + W2 + W3,
    W0 * (W1 + W2 + W3) + W1 * SUM2 + W2 * W3,
    W0 * (W1 * W2 + W1 * W3 + W2 * W3) + W1 * PROD2,
    W0 * W1 * W2 * W3,
)


def even_pairs(count):
    return [(i, i ^ 1) for i in range(count)]


def odd_pairs(count):
    return [(i, (i + 1) % count if i % 2 else (i - 1) % count) for i in range(count)]


def shape_of(*dims):
    return jax.ShapeDtypeStruct(dims, F32)


IN_PLACE = pl.BlockSpec(memory_space=pltpu.VMEM)
ANYWHERE = pl.BlockSpec(memory_space=pltpu.HBM)


def call(kernel, outs, *args, in_specs=None, out_specs=None, scratch=(), aliases=None, cost=0):
    many = isinstance(outs, (list, tuple))
    return pl.pallas_call(
        kernel,
        out_shape=outs,
        in_specs=in_specs or [IN_PLACE] * len(args),
        out_specs=out_specs or ([IN_PLACE] * len(outs) if many else IN_PLACE),
        scratch_shapes=scratch,
        input_output_aliases=aliases or {},
        cost_estimate=pl.CostEstimate(flops=cost, bytes_accessed=cost, transcendentals=0),
        compiler_params=pltpu.CompilerParams(vmem_limit_bytes=12 << 20),
    )(*args)


def tile_at(tile):
    return pl.ds(pl.multiple_of(tile * LANES, LANES), LANES)


def each_tile(width, work, unroll=4):
    def step(tile, carry):
        work(tile, tile_at(tile))
        return carry

    tiles = width // LANES
    lax.fori_loop(0, tiles, step, 0, unroll=min(unroll, tiles))


def iota(rows, dim):
    return lax.broadcasted_iota(jnp.int32, (rows, LANES), dim)


def down(cells, by):
    return pltpu.roll(cells, by, 0)


def around(ref, index, tile, tiles, circular=True):
    cells = ref[index, :, tile_at(tile)]
    before = ref[index, :, tile_at(lax.rem(tile + tiles - 1, tiles))]
    after = ref[index, :, tile_at(lax.rem(tile + 1, tiles))]
    lane = iota(cells.shape[0], 1)
    west = pltpu.roll(jnp.where(lane == LANES - 1, before, cells), 1, 1)
    east = pltpu.roll(jnp.where(lane == 0, after, cells), LANES - 1, 1)
    return cells, west + east + (down(cells, 1) + down(cells, cells.shape[0] - 1))


def places(tm_count):
    t = lax.axis_index("tm")
    odd = lax.rem(t, 2)
    return odd, jnp.where(odd == 1, t < tm_count - 1, t > 0).astype(F32)


def lat_places(lat_count):
    l = lax.axis_index("lat")
    return lax.rem(l, 2) == 0, (l < lat_count - 1).astype(F32), (l > 0).astype(F32)


def mirrored(odd, j):
    return jnp.where(odd == 1, SLICES - 1 - j, j)


def first_kernel(cot, _, own, la, lb, e3, *o3):
    odd, _ = places(2)
    even_lat, _, _ = lat_places(2)
    for j in range(SLICES):
        own[j] = cot[pl.ds(mirrored(odd, j), 1)][0]
    e3[...] = own[1]
    if o3:
        o3[0][...] = own[2]
    sub = iota(8, 0)

    def work(tile, cols):
        for i in range(0, SLICES, 2):
            first = jnp.where(sub < 4, own[i, :8, cols], down(own[i + 1, :8, cols], 5))
            last = jnp.where(sub >= 4, own[i, ROWS - 8 :, cols], down(own[i + 1, ROWS - 8 :, cols], 3))
            at = pl.ds(4 * i, 8)
            la[at, cols] = jnp.where(even_lat, last, first)
            lb[at, cols] = jnp.where(even_lat, first, last)

    each_tile(own.shape[2], work)


def in_blocks(out, cells):
    chunk = out.shape[1]
    blocks = cells.shape[1] // chunk
    for b in range(blocks):
        out[b * ROWS : (b + 1) * ROWS] = cells[:, b * chunk : (b + 1) * chunk]
    return blocks * ROWS


def near_kernel(near_e, near_o, rng, e1, o1):
    for out, cells in ((e1, near_e), (o1, near_o)):
        out[in_blocks(out, cells) :] = rng[...]


def below_above(lat_count, la, lb, at, cols):
    even_lat, has_below, has_above = lat_places(lat_count)
    a, b = la[pl.ds(at, 8), cols], lb[pl.ds(at, 8), cols]
    return jnp.where(even_lat, a, b) * has_below, jnp.where(even_lat, b, a) * has_above


def edge_rows(blocks):
    return (2 * blocks + 7) // 8 * 8


def far_kernel(lat_count, own, la, lb, *refs):
    e2, o2 = refs[-2:]
    chunk = e2.shape[1]
    blocks = own.shape[2] // chunk
    sub = iota(8, 0)
    for out, j, at, shifts in ((o2, 1, 0, (3, 5)), (e2, 2, 8, (0, 0))):
        start = in_blocks(out, own.at[j])
        for tile in range(chunk // LANES):
            for v in range(0, edge_rows(blocks), 8):
                rows = jnp.zeros((8, LANES), F32)
                for k in range(4):
                    b = v // 2 + k
                    if b < blocks:
                        cols = pl.ds(b * chunk + tile * LANES, LANES)
                        below, above = below_above(lat_count, la, lb, at, cols)
                        below = down(below, (shifts[0] + 2 * k + 1) % 8)
                        above = down(above, (shifts[1] + 2 * k + 1) % 8)
                        rows = jnp.where(sub == 2 * k, above, jnp.where(sub == 2 * k + 1, below, rows))
                out[start + v : start + v + 8, tile * LANES : (tile + 1) * LANES] = rows


def slab(ref, tile):
    per = ref.shape[1] // LANES
    at = pl.multiple_of(lax.div(tile, per) * ROWS, ROWS)
    return ref[pl.ds(at, ROWS), tile_at(lax.rem(tile, per))]


def rows_kernel(forward, e1, o1, *refs):
    chunk = e1.shape[1]
    even_lat, _, _ = lat_places(2)
    if forward:
        rng, far, la, lb, full = refs
        t = lax.axis_index("tm")
        for piece, owner in (
            (rng[...], t),
            (e1[pl.ds(e1.shape[0] - ROWS, ROWS)], t ^ 1),
            (far[...], t ^ 2),
            (o1[pl.ds(e1.shape[0] - ROWS, ROWS)], t ^ 3),
        ):
            full[:, pl.ds(pl.multiple_of(owner * chunk, chunk), chunk)] = piece
    else:
        gathered, la, lb, full = refs
        full[...] = gathered[...]
    sub = iota(8, 0)

    def work(tile, cols):
        near_e, near_o, field = slab(e1, tile), slab(o1, tile), full[:, cols]
        first = jnp.where(sub < 2, near_e[:8], jnp.where(sub < 4, down(near_o[:8], 2), down(field[:8], 4)))
        last = jnp.where(sub >= 6, near_e[8:], jnp.where(sub >= 4, down(near_o[8:], 6), down(field[8:], 4)))
        la[:, cols] = jnp.where(even_lat, last, first)
        lb[:, cols] = jnp.where(even_lat, first, last)

    each_tile(full.shape[1], work)


def main_kernel(counts, forward, own, e1, o1, e2, o2, full, la1, lb1, la2, lb2, its, u, y1, y2, rr, *grads):
    tm_count, lat_count = counts
    odd, has_before = places(tm_count)
    _, has_below, has_above = lat_places(lat_count)
    width = own.shape[2]
    chunk = e2.shape[1]
    tiles = width // LANES
    sub = iota(8, 0)
    row = iota(HELD, 0)
    mask = jnp.where(row < ROWS, 1.0, jnp.where(row < ROWS + 4, has_below, has_above))
    grad = grads[-1]

    def gather(tile, cols):
        def joined(cells, below, above):
            return jnp.concatenate([cells, jnp.where(sub < 4, below, above)], axis=0)

        for i in range(0, SLICES, 2):
            below, above = below_above(lat_count, la1, lb1, 4 * i, cols)
            u[1 + i, :, cols] = joined(own[i, :, cols], below, above)
            u[2 + i, :, cols] = joined(own[i + 1, :, cols], down(below, 3), down(above, 5))
        below, above = below_above(lat_count, la2, lb2, 0, cols)
        u[0, :, cols] = joined(slab(o1, tile), down(below, 6), down(above, 2)) * has_before
        u[SLICES + 1, :, cols] = joined(slab(e1, tile), below, above)
        rr[:, cols] = joined(full[:, cols], down(below, 4), down(above, 4)) + 6.0

    each_tile(width, gather)

    def once(tile, cols):
        field = rr[:, cols]
        for i in range(SLICES + 2):
            cells, beside = around(u, i, tile, tiles)
            y1[i, :, cols] = (beside - field * cells) * mask

    each_tile(width, once)

    def twice(tile, cols):
        field = rr[:, cols]
        c0 = [u[i, :ROWS, cols] for i in range(SLICES + 2)]
        c1 = [y1[i, :ROWS, cols] for i in range(SLICES + 2)]
        total = jnp.zeros((ROWS, LANES), F32)
        for j in range(SLICES):
            cells, beside = around(y1, j + 1, tile, tiles)
            out = (beside - field * cells) * mask
            y2[j, :, cols] = out
            at = mirrored(odd, j)
            x1, x2, x3 = (its[k, pl.ds(at, 1), :, cols][0] for k in range(3))
            one = c1[j + 1] + (c0[j] + c0[j + 2])
            two = out[:ROWS] + 2.0 * (c1[j] + c1[j + 2])
            two = two + (1.0 + (has_before if j == 0 else 1.0)) * c0[j + 1]
            two = two + (c0[j - 1] if j > 0 else slab(o2, tile) * has_before)
            two = two + (c0[j + 3] if j < SLICES - 1 else slab(e2, tile))
            total = total + c0[j + 1] * (W3 * x3 + W2 * x2 + W1 * x1)
            total = total + one * ((W2 * W3) * x2 + (W1 * SUM2) * x1) + two * ((W1 * PROD2) * x1)
        grad[:, cols] = -total

    each_tile(width, twice)
    if forward:
        t = lax.axis_index("tm")
        passed = width // chunk * ROWS
        for i, out in enumerate(grads[:4]):
            at = passed if i == 2 else 0
            out[at:] = grad[:, pl.ds(pl.multiple_of((t ^ i) * chunk, chunk), chunk)]
        grads[2][:passed] = e2[:passed]


def noise_kernel(tm_count, u, y1, y2, rr, e2, o2, e3, noise, ends, part, beside_far, sems):
    odd, has_before = places(tm_count)
    width = part.shape[2]
    tiles = width // LANES
    K0, K1, K2, K3 = COEFFS
    chunk = e2.shape[1]
    blocks = width // chunk
    row = iota(ROWS, 0)
    sub = iota(8, 0)
    for i, ref in enumerate((o2, e2)):
        for b in range(blocks):
            for tile in range(chunk // LANES):
                at = blocks * ROWS + b // 4 * 8
                rows = ref[at : at + 8, tile * LANES : (tile + 1) * LANES]
                k = b % 4
                rows = jnp.where(sub < 4, down(rows, (8 - 2 * k) % 8), down(rows, 6 - 2 * k))
                beside_far[i, :, b * chunk + tile * LANES : b * chunk + (tile + 1) * LANES] = rows

    def work(tile, cols):
        field = rr[:ROWS, cols]
        c0 = [u[i, :ROWS, cols] for i in range(SLICES + 2)]
        c1, c2, c3 = [], [], []
        for i in range(SLICES + 2):
            if i in (0, SLICES + 1):
                cells, beside = around(y1, i, tile, tiles)
                c1.append(cells[:ROWS])
                c2.append(beside[:ROWS] - field * cells[:ROWS])
                c3.append(None)
            else:
                cells, beside = around(y2, i - 1, tile, tiles)
                c1.append(y1[i, :ROWS, cols])
                c2.append(cells[:ROWS])
                c3.append(beside[:ROWS] - field * cells[:ROWS])
        far = []
        lane = iota(ROWS, 1)
        for i, ref in enumerate((o2, e2)):
            cells = slab(ref, tile)
            before = slab(ref, lax.rem(tile + tiles - 1, tiles))
            after = slab(ref, lax.rem(tile + 1, tiles))
            west = pltpu.roll(jnp.where(lane == LANES - 1, before, cells), 1, 1)
            east = pltpu.roll(jnp.where(lane == 0, after, cells), LANES - 1, 1)
            edge = jnp.concatenate([beside_far[i, :, cols]] * 2, axis=0)
            above = jnp.where(row == 0, edge, down(cells, 1))
            below = jnp.where(row == ROWS - 1, edge, down(cells, ROWS - 1))
            once = west + east + (above + below) - field * cells
            scale = has_before if i == 0 else 1.0
            far.append((cells * scale, once * scale))
        c0 = [far[0][0], *c0, far[1][0]]
        c1 = [far[0][1], *c1, far[1][1]]
        back = (1.0 + has_before, 2.0 + has_before)
        for j in range(SLICES):
            a, b = j + 2, j + 1
            one = c1[a] + (c0[a - 1] + c0[a + 1])
            twofold = back[0] if j == 0 else 2.0
            two = c2[b] + 2.0 * (c1[a - 1] + c1[a + 1]) + (c0[a - 2] + twofold * c0[a] + c0[a + 2])
            three = c3[b] + 3.0 * (c2[b - 1] + c2[b + 1] + (c1[a - 2] + twofold * c1[a] + c1[a + 2]))
            left = back[1] if j == 1 else 3.0
            right = back[1] if j == 0 else 3.0
            three = three + left * c0[a - 1] + right * c0[a + 1]
            if j > 0:
                three = three + c0[a - 3]
            three = three + (c0[a + 3] if j < SLICES - 1 else e3[:, cols])
            out = K0 * c0[a] + K1 * one + K2 * two + K3 * three
            if j == 0:
                ends[:, cols] = out
            else:
                part[j - 1, :, cols] = out

    each_tile(width, work)
    copies = [
        pltpu.make_async_copy(part.at[j - 1], noise.at[mirrored(odd, j)], sems.at[j])
        for j in range(1, SLICES)
    ]
    for copy in copies:
        copy.start()
    for copy in copies:
        copy.wait()


def last_kernel(tm_count, forward, noise_in, ends, o3, *refs):
    *parts, noise, gradient, part, sems = refs
    odd, has_before = places(tm_count)

    def work(tile, cols):
        part[:, cols] = ends[:, cols] + (COEFFS[3] * has_before) * (slab(o3, tile) if forward else o3[:, cols])

    each_tile(part.shape[1], work)
    copy = pltpu.make_async_copy(part, noise.at[mirrored(odd, 0)], sems.at[0])
    copy.start()
    total = parts[0][...]
    for more in parts[1:]:
        total = total + more[...]
    if forward:
        total = total + o3[pl.ds(o3.shape[0] - ROWS, ROWS)]
    gradient[...] = total
    copy.wait()


def body(counts, cotangent, iterates, range_field):
    tm_count, lat_count = counts
    forward = tm_count == 4
    slices, rows, width = cotangent.shape
    chunk = range_field.shape[1]
    assert slices == SLICES and rows == ROWS
    even, odd = even_pairs(tm_count), odd_pairs(tm_count)
    lat_even, lat_odd = even_pairs(lat_count), odd_pairs(lat_count)
    y_pairs = [(i, i ^ 2) for i in range(tm_count)]
    one = shape_of(ROWS, width)
    dma = pltpu.SemaphoreType.DMA

    blocks = width // chunk
    message = shape_of((blocks + 1) * ROWS, chunk)
    flip = lax.rem(lax.axis_index("tm"), 2) == 1
    near_e, near_o = (
        lax.dynamic_index_in_dim(cotangent, jnp.where(flip, SLICES - 1 - j, j), 0, False)
        for j in (SLICES - 1, 0)
    )
    e1, o1 = call(near_kernel, [message, message], near_e, near_o, range_field)
    e1 = lax.ppermute(e1, "tm", even)
    o1 = lax.ppermute(o1, "tm", odd)
    if forward:
        field = (range_field, lax.ppermute(range_field, "tm", y_pairs))
    else:
        field = (lax.all_gather(range_field, "tm", axis=1, tiled=True),)
    own, la1, lb1, e3, *o3 = call(
        first_kernel, [shape_of(SLICES, ROWS, width)] + [one] * (3 if forward else 4), cotangent, field[-1]
    )
    la1 = lax.ppermute(la1, "lat", lat_even)
    lb1 = lax.ppermute(lb1, "lat", lat_odd)
    far = shape_of(blocks * ROWS + edge_rows(blocks), chunk)
    e2, o2 = call(functools.partial(far_kernel, lat_count), [far, far], own, la1, lb1, e1)
    e2 = lax.ppermute(e2, "tm", even)
    o2 = lax.ppermute(o2, "tm", odd)
    e3 = lax.ppermute(e3, "tm", even)

    edge = shape_of(8, width)
    la2, lb2, full = call(functools.partial(rows_kernel, forward), [edge, edge, one], e1, o1, *field)
    la2 = lax.ppermute(la2, "lat", lat_even)
    lb2 = lax.ppermute(lb2, "lat", lat_odd)
    held = shape_of(SLICES + 2, HELD, width)
    outs = [held, held, shape_of(SLICES, HELD, width), shape_of(HELD, width)]
    piece = shape_of(ROWS, chunk)
    u, y1, y2, rr, *parts = call(
        functools.partial(main_kernel, counts, forward),
        outs + ([piece, piece, message, piece] if forward else [one]),
        own,
        e1,
        o1,
        e2,
        o2,
        full,
        la1,
        lb1,
        la2,
        lb2,
        iterates,
        scratch=[pltpu.VMEM((ROWS, width), F32)] if forward else (),
    )
    if forward:
        g0, g1, g2, g3 = parts
        o3 = lax.ppermute(g2, "tm", y_pairs)
        g1 = lax.ppermute(g1, "tm", even)
        g3 = lax.ppermute(g3, "tm", odd)
        parts = (g0, g1, g3)
    else:
        o3 = lax.ppermute(o3[0], "tm", odd)
        parts = (lax.psum_scatter(parts[0], "tm", scatter_dimension=1, tiled=True),)

    noise, ends = call(
        functools.partial(noise_kernel, tm_count),
        [shape_of(SLICES, ROWS, width), one],
        u,
        y1,
        y2,
        rr,
        e2,
        o2,
        e3,
        out_specs=[ANYWHERE, IN_PLACE],
        scratch=[pltpu.VMEM((SLICES - 1, ROWS, width), F32), pltpu.VMEM((2, 8, width), F32), dma((SLICES,))],
    )
    return call(
        functools.partial(last_kernel, tm_count, forward),
        [shape_of(SLICES, ROWS, width), shape_of(ROWS, chunk)],
        noise,
        ends,
        o3,
        *parts,
        in_specs=[ANYWHERE] + [IN_PLACE] * (2 + len(parts)),
        out_specs=[ANYWHERE, IN_PLACE],
        scratch=[pltpu.VMEM((ROWS, width), F32), dma((1,))],
        aliases={0: 0},
    )


def solution(mesh):
    counts = (mesh.shape["tm"], mesh.shape["lat"])
    return jax.shard_map(
        functools.partial(body, counts),
        mesh=mesh,
        in_specs=(P("tm", "lat", None), P(None, "tm", "lat", None), P("lat", "tm")),
        out_specs=(P("tm", "lat", None), P("lat", "tm")),
        check_vma=False,
    )
```

```python
import functools
import math

import jax
import jax.numpy as jnp
from jax import lax
from jax.experimental import pallas as pl
from jax.experimental.pallas import tpu as pltpu
from jax.sharding import PartitionSpec as P

F32 = jnp.float32
LANES = 128
SLICES = 4
ROWS = 16
HELD = 24


def step_weights():
    centre_value = 6.525
    spread_value = 6.475
    root_order = (3, 0, 2, 1)
    return [
        1.0 / (centre_value + spread_value * math.cos(math.pi * (2 * section + 1) / 8.0))
        for section in root_order
    ]


W0, W1, W2, W3 = step_weights()
SUM2 = W2 + W3
PROD2 = W2 * W3
COEFFS = (
    W0 + W1 + W2 + W3,
    W0 * (W1 + W2 + W3) + W1 * SUM2 + W2 * W3,
    W0 * (W1 * W2 + W1 * W3 + W2 * W3) + W1 * PROD2,
    W0 * W1 * W2 * W3,
)


def even_pairs(count):
    return [(i, i ^ 1) for i in range(count)]


def odd_pairs(count):
    return [(i, (i + 1) % count if i % 2 else (i - 1) % count) for i in range(count)]


def lat_odd_pairs(count):
    return [(i, i if i in (0, count - 1) else other) for i, other in odd_pairs(count)]


def shape_of(*dims):
    return jax.ShapeDtypeStruct(dims, F32)


IN_PLACE = pl.BlockSpec(memory_space=pltpu.VMEM)
ANYWHERE = pl.BlockSpec(memory_space=pltpu.HBM)


def call(kernel, outs, *args, in_specs=None, out_specs=None, scratch=(), aliases=None, cost=0):
    many = isinstance(outs, (list, tuple))
    return pl.pallas_call(
        kernel,
        out_shape=outs,
        in_specs=in_specs or [IN_PLACE] * len(args),
        out_specs=out_specs or ([IN_PLACE] * len(outs) if many else IN_PLACE),
        scratch_shapes=scratch,
        input_output_aliases=aliases or {},
        cost_estimate=pl.CostEstimate(flops=cost, bytes_accessed=cost, transcendentals=0),
        compiler_params=pltpu.CompilerParams(vmem_limit_bytes=12 << 20),
    )(*args)


def tile_at(tile):
    return pl.ds(pl.multiple_of(tile * LANES, LANES), LANES)


def each_tile(width, work, unroll=8):
    def step(tile, carry):
        work(tile, tile_at(tile))
        return carry

    tiles = width // LANES
    lax.fori_loop(0, tiles, step, 0, unroll=min(unroll, tiles))


def iota(rows, dim):
    return lax.broadcasted_iota(jnp.int32, (rows, LANES), dim)


def down(cells, by):
    return pltpu.roll(cells, by, 0)


def around(ref, index, tile, tiles, circular=True):
    cells = ref[index, :, tile_at(tile)]
    before = ref[index, :, tile_at(lax.rem(tile + tiles - 1, tiles))]
    after = ref[index, :, tile_at(lax.rem(tile + 1, tiles))]
    lane = iota(cells.shape[0], 1)
    west = pltpu.roll(jnp.where(lane == LANES - 1, before, cells), 1, 1)
    east = pltpu.roll(jnp.where(lane == 0, after, cells), LANES - 1, 1)
    return cells, west + east + (down(cells, 1) + down(cells, cells.shape[0] - 1))


def places(tm_count):
    t = lax.axis_index("tm")
    odd = lax.rem(t, 2)
    return odd, jnp.where(odd == 1, t < tm_count - 1, t > 0).astype(F32)


def lat_places(lat_count):
    l = lax.axis_index("lat")
    return lax.rem(l, 2) == 0, (l < lat_count - 1).astype(F32), (l > 0).astype(F32)


def mirrored(odd, j):
    return jnp.where(odd == 1, SLICES - 1 - j, j)


def first_kernel(cot, *slabs):
    odd, _ = places(2)
    for j in range(SLICES):
        slabs[j][...] = cot[pl.ds(mirrored(odd, j), 1)][0]


def scale_kernel(s2, rng, its, far_e, held, scales):
    far_e[...] = s2[...]
    held[...] = rng[...]
    odd, _ = places(2)

    def work(tile, cols):
        for j in range(SLICES):
            x1, x2, x3 = (its[k, pl.ds(mirrored(odd, j), 1), :, cols][0] for k in range(3))
            scales[0, j, :, cols] = W3 * x3 + W2 * x2 + W1 * x1
            scales[1, j, :, cols] = (W2 * W3) * x2 + (W1 * SUM2) * x1
            scales[2, j, :, cols] = (W1 * PROD2) * x1

    each_tile(s2.shape[1], work)


def rows_kernel(forward, *refs):
    slabs, (near_e, near_o), refs = refs[:SLICES], refs[SLICES : SLICES + 2], refs[SLICES + 2 :]
    even_lat, _, _ = lat_places(2)
    *field, full, la, lb = refs
    if forward:
        t = lax.axis_index("tm")
        chunk = field[0].shape[1]
        for i, piece in enumerate(field):
            full[:, pl.ds(pl.multiple_of((t ^ i) * chunk, chunk), chunk)] = piece[...]
    else:
        full[...] = field[0][...]
    sub = iota(8, 0)

    def work(tile, cols):
        for i in range(SLICES // 2):
            one, two, field = slabs[2 * i], slabs[2 * i + 1], full
            first = jnp.where(sub == 3, down(field[:8, cols], 3 - i), down(two[:8, cols], 5))
            first = jnp.where(sub < 3, one[:8, cols], first)
            last = jnp.where(sub == 4, down(field[8:, cols], 6 - i), down(two[8:, cols], 3))
            last = jnp.where(sub > 4, one[8:, cols], last)
            la[8 * i : 8 * i + 8, cols] = jnp.where(even_lat, last, first)
            lb[8 * i : 8 * i + 8, cols] = jnp.where(even_lat, first, last)
        first = jnp.where(sub < 2, near_e[:8, cols], down(near_o[:8, cols], 2))
        last = jnp.where(sub >= 6, near_e[8:, cols], down(near_o[8:, cols], 6))
        la[16:, cols] = jnp.where(even_lat, last, first)
        lb[16:, cols] = jnp.where(even_lat, first, last)

    each_tile(full.shape[1], work)


def below_above(lat_count, la, lb, at, cols):
    even_lat, has_below, has_above = lat_places(lat_count)
    a, b = la[pl.ds(at, 8), cols], lb[pl.ds(at, 8), cols]
    return jnp.where(even_lat, a, b) * has_below, jnp.where(even_lat, b, a) * has_above


def joined(cells, below, above):
    return jnp.concatenate([cells, jnp.where(iota(8, 0) < 4, below, above)], axis=0)


def lat_mask(lat_count):
    _, has_below, has_above = lat_places(lat_count)
    row = iota(HELD, 0)
    return jnp.where(row < ROWS, 1.0, jnp.where(row < ROWS + 4, has_below, has_above))


def at(cells, j):
    return cells[j] if 0 <= j < SLICES else 0.0


def own_kernel(counts, s0, s1, s2, s3, full, la, lb, scales, grad, noise, rr, edge_e, edge_o, u, y1, y2):
    tm_count, lat_count = counts
    K0, K1, K2, _ = COEFFS
    odd, has_before = places(tm_count)
    width = full.shape[1]
    tiles = width // LANES
    mask = lat_mask(lat_count)
    back = 1.0 + has_before

    def gather(tile, cols):
        first, last = below_above(lat_count, la, lb, 0, cols)
        second, ahead = below_above(lat_count, la, lb, 8, cols)
        u[0, :, cols] = joined(s0[:, cols], first, last)
        u[1, :, cols] = joined(s1[:, cols], down(first, 3), down(last, 5))
        u[2, :, cols] = joined(s2[:, cols], second, ahead)
        u[3, :, cols] = joined(s3[:, cols], down(second, 3), down(ahead, 5))
        sub = iota(8, 0)
        below = jnp.where(sub == 0, down(first, 5), down(second, 6))
        above = jnp.where(sub == 7, down(ahead, 3), down(last, 2))
        rr[:, cols] = joined(full[:, cols], below, above) + 6.0

    each_tile(width, gather)

    def once(tile, cols):
        field = rr[:, cols]
        for j in range(SLICES):
            cells, beside = around(u, j, tile, tiles)
            y1[j, :, cols] = (beside - field * cells) * mask

    each_tile(width, once)

    def twice(tile, cols):
        field = rr[:, cols]
        c0 = [u[j, :ROWS, cols] for j in range(SLICES)]
        c1 = [y1[j, :ROWS, cols] for j in range(SLICES)]
        total = jnp.zeros((ROWS, LANES), F32)
        for j in range(SLICES):
            cells, beside = around(y1, j, tile, tiles)
            c2 = (beside - field * cells) * mask
            y2[j, :, cols] = c2
            one = c1[j] + (at(c0, j - 1) + at(c0, j + 1))
            two = c2[:ROWS] + 2.0 * (at(c1, j - 1) + at(c1, j + 1))
            two = two + (back if j == 0 else 2.0) * c0[j] + (at(c0, j - 2) + at(c0, j + 2))
            total = total + c0[j] * scales[0, j, :, cols] + one * scales[1, j, :, cols] + two * scales[2, j, :, cols]
            noise[j, :, cols] = K0 * c0[j] + K1 * one + K2 * two
        grad[:, cols] = -total

    each_tile(width, twice)
    chunk = edge_e.shape[1]
    blocks = width // chunk
    sub = iota(8, 0)
    for out, start, shifts in ((edge_o, 0, (3, 5)), (edge_e, 8, (0, 0))):
        for tile in range(chunk // LANES):
            for v in range(0, edge_rows(blocks), 8):
                rows = jnp.zeros((8, LANES), F32)
                for k in range(min(4, blocks - v // 2)):
                    cols = pl.ds((v // 2 + k) * chunk + tile * LANES, LANES)
                    below, above = below_above(lat_count, la, lb, start, cols)
                    below = down(below, (shifts[0] + 2 * k + 1) % 8)
                    above = down(above, (shifts[1] + 2 * k + 1) % 8)
                    rows = jnp.where(sub == 2 * k, above, jnp.where(sub == 2 * k + 1, below, rows))
                out[v : v + 8, tile * LANES : (tile + 1) * LANES] = rows


def third_kernel(tm_count, noise, u, y1, y2, rr, _, out):
    _, has_before = places(tm_count)
    width = noise.shape[2]
    tiles = width // LANES
    K3 = COEFFS[3]
    back = 1.0 + has_before

    def thrice(tile, cols):
        field = rr[:ROWS, cols]
        c0 = [u[j, :ROWS, cols] for j in range(SLICES)]
        c1 = [y1[j, :ROWS, cols] for j in range(SLICES)]
        c2 = [y2[j, :ROWS, cols] for j in range(SLICES)]
        for j in range(SLICES):
            cells, beside = around(y2, j, tile, tiles)
            three = beside[:ROWS] - field * cells[:ROWS]
            three = three + 3.0 * (at(c2, j - 1) + at(c2, j + 1) + at(c1, j - 2) + at(c1, j + 2))
            three = three + (3.0 * back if j == 0 else 6.0) * c1[j]
            left, right = (1.0 + back if j == i else 3.0 for i in (1, 0))
            three = three + (left * at(c0, j - 1) + right * at(c0, j + 1) + at(c0, j - 3) + at(c0, j + 3))
            out[j, :, cols] = noise[j, :, cols] + K3 * three

    each_tile(width, thrice)


def edge_rows(blocks):
    return (2 * blocks + 7) // 8 * 8


def near_kernel(counts, forward, grad, near_e, near_o, far_e, far_o, la, lb, rr, edge_e, edge_o, scales, *refs):
    tm_count, lat_count = counts
    odd, has_before = places(tm_count)
    width = grad.shape[1]
    tiles = width // LANES
    mask = lat_mask(lat_count)
    u, y1 = refs[:2]
    total = refs[-1] if forward else refs[2]

    def gather(tile, cols):
        below, above = below_above(lat_count, la, lb, 16, cols)
        u[0, :, cols] = joined(near_o[:, cols], down(below, 6), down(above, 2)) * has_before
        u[1, :, cols] = joined(near_e[:, cols], below, above)

    each_tile(width, gather)

    def once(tile, cols):
        field = rr[:, cols]
        out = grad[:, cols]
        for i, far in enumerate((far_o, far_e)):
            cells, beside = around(u, i, tile, tiles)
            c1 = (beside - field * cells) * mask
            y1[i, :, cols] = c1
            beyond = far[:, cols] * has_before if i == 0 else far[:, cols]
            j, inner = (0, 1) if i == 0 else (SLICES - 1, SLICES - 2)
            add = cells[:ROWS] * (scales[1, j, :, cols] + scales[2, inner, :, cols])
            out = out - (add + (2.0 * c1[:ROWS] + beyond) * scales[2, j, :, cols])
        total[:, cols] = out

    each_tile(width, once, unroll=2)
    if forward:
        t = lax.axis_index("tm")
        chunk = refs[2].shape[1]
        for i, out in enumerate(refs[2:6]):
            out[:ROWS] = total[:, pl.ds(pl.multiple_of((t ^ i) * chunk, chunk), chunk)]
        refs[3][ROWS:] = edge_e[...]
        refs[5][ROWS:] = edge_o[...]
def last_kernel(tm_count, own, u, y1, rr, far_e, far_o, end_e, end_o, edge_e, edge_o, *refs):
    *parts, noise, gradient, out, total, beside_far, sems = refs
    odd, has_before = places(tm_count)
    width = own.shape[2]
    tiles = width // LANES
    K0, K1, K2, K3 = COEFFS
    chunk = total.shape[1]
    for i, more in enumerate(parts):
        total[...] = more[:ROWS] if i == 0 else total[...] + more[:ROWS]
    copies = [pltpu.make_async_copy(total, gradient, sems.at[0])]
    copies[0].start()
    blocks = width // chunk
    start = edge_e.shape[0] - edge_rows(blocks)
    sub = iota(8, 0)
    for i, ref in enumerate((edge_o, edge_e)):
        for b in range(blocks):
            for tile in range(chunk // LANES):
                k, at = b % 4, start + b // 4 * 8
                rows = ref[at : at + 8, tile * LANES : (tile + 1) * LANES]
                rows = jnp.where(sub < 4, down(rows, (8 - 2 * k) % 8), down(rows, 6 - 2 * k))
                beside_far[i, :, b * chunk + tile * LANES : b * chunk + (tile + 1) * LANES] = rows
    row, lane = iota(ROWS, 0), iota(ROWS, 1)

    def work(tile, cols):
        field = rr[:ROWS, cols]
        result = [own[j, :, cols] for j in range(SLICES)]
        for i, (far, end) in enumerate(((far_o, end_o), (far_e, end_e))):
            cells, beside = around(y1, i, tile, tiles)
            n0, n1 = u[i, :ROWS, cols], cells[:ROWS]
            n2 = beside[:ROWS] - field * n1
            f0 = far[:, cols]
            before = far[:, tile_at(lax.rem(tile + tiles - 1, tiles))]
            after = far[:, tile_at(lax.rem(tile + 1, tiles))]
            west = pltpu.roll(jnp.where(lane == LANES - 1, before, f0), 1, 1)
            east = pltpu.roll(jnp.where(lane == 0, after, f0), LANES - 1, 1)
            edge = jnp.concatenate([beside_far[i, :, cols]] * 2, axis=0)
            above = jnp.where(row == 0, edge, down(f0, 1))
            below = jnp.where(row == ROWS - 1, edge, down(f0, ROWS - 1))
            f1 = west + east + (above + below) - field * f0
            beyond = 3.0 * f1 + end[:, cols]
            if i == 0:
                f0, beyond = f0 * has_before, beyond * has_before
            a, b, c = (0, 1, 2) if i == 0 else (3, 2, 1)
            result[a] = result[a] + (K1 + 3.0 * K3) * n0 + K2 * (2.0 * n1 + f0) + K3 * (3.0 * n2 + beyond)
            result[b] = result[b] + K2 * n0 + K3 * (3.0 * n1 + f0)
            result[c] = result[c] + K3 * n0
        for j in range(SLICES):
            out[j, :, cols] = result[j]

    per = min(4, tiles)
    for q in range(0, tiles, per):

        def step(tile, carry):
            work(tile, tile_at(tile))
            return carry

        lax.fori_loop(q, q + per, step, 0, unroll=per)
        cols = pl.ds(q * LANES, per * LANES)
        for j in range(SLICES):
            copy = pltpu.make_async_copy(
                out.at[j, :, cols], noise.at[mirrored(odd, j), :, cols], sems.at[1 + q // per * SLICES + j]
            )
            copy.start()
            copies.append(copy)
    for copy in copies:
        copy.wait()


def body(counts, cotangent, iterates, range_field):
    tm_count, lat_count = counts
    forward = tm_count == 4
    slices, rows, width = cotangent.shape
    chunk = range_field.shape[1]
    assert slices == SLICES and rows == ROWS
    even, odd = even_pairs(tm_count), odd_pairs(tm_count)
    lat_even, lat_odd = even_pairs(lat_count), lat_odd_pairs(lat_count)
    y_pairs = [(i, i ^ 2) for i in range(tm_count)]
    one = shape_of(ROWS, width)
    extra = edge_rows(width // chunk)

    if forward:
        field = [range_field] + [lax.ppermute(range_field, "tm", pairs) for pairs in (even, y_pairs, odd)]
    else:
        field = [lax.all_gather(range_field, "tm", axis=1, tiled=True)]
    s0, s1, s2, s3 = slabs = call(first_kernel, [one] * SLICES, cotangent)
    near_e, near_o = lax.ppermute(s3, "tm", even), lax.ppermute(s0, "tm", odd)
    far_e, held, scales = call(
        scale_kernel, [one, shape_of(ROWS, chunk), shape_of(3, SLICES, ROWS, width)], s2, range_field, iterates
    )
    if forward:
        field[0] = held
    pair = shape_of(24, width)
    full, la1, lb1 = call(functools.partial(rows_kernel, forward), [one, pair, pair], *slabs, near_e, near_o, *field)
    la1, lb1 = lax.ppermute(la1, "lat", lat_even), lax.ppermute(lb1, "lat", lat_odd)
    far_e, far_o = lax.ppermute(far_e, "tm", even), lax.ppermute(s1, "tm", odd)
    end_e = lax.ppermute(s1, "tm", even)
    end_o = lax.ppermute(far_e, "tm", y_pairs) if forward else lax.ppermute(s2, "tm", odd)

    deep = shape_of(SLICES, HELD, width)
    own = shape_of(SLICES, ROWS, width)
    edge = shape_of(extra, chunk)
    grad, own, rr, edge_e, edge_o, *powers = call(
        functools.partial(own_kernel, counts),
        [one, own, shape_of(HELD, width), edge, edge, deep, deep, deep],
        *slabs,
        full,
        la1,
        lb1,
        scales,
    )
    two = shape_of(2, HELD, width)
    if forward:
        outs = [shape_of(ROWS + more, chunk) for more in (0, extra, 0, extra)]
    else:
        outs = [one]
    u, y1, *outs = call(
        functools.partial(near_kernel, counts, forward),
        [two, two] + outs,
        grad,
        near_e,
        near_o,
        far_e,
        far_o,
        la1,
        lb1,
        rr,
        edge_e,
        edge_o,
        scales,
        scratch=[pltpu.VMEM((ROWS, width), F32)] if forward else (),
    )
    own = call(
        functools.partial(third_kernel, tm_count), shape_of(SLICES, ROWS, width), own, *powers, rr, u
    )
    if forward:
        g1, g2, g3 = (lax.ppermute(g, "tm", p) for g, p in zip(outs[1:], (even, y_pairs, odd)))
        edge_e, edge_o = g1, g3
        parts = (outs[0], g1, g2, g3)
    else:
        parts = (lax.psum_scatter(outs[0], "tm", scatter_dimension=1, tiled=True),)
        edge_e, edge_o = lax.ppermute(edge_e, "tm", even), lax.ppermute(edge_o, "tm", odd)
    tiles = width // LANES
    return call(
        functools.partial(last_kernel, tm_count),
        [shape_of(SLICES, ROWS, width), shape_of(ROWS, chunk)],
        own,
        u,
        y1,
        rr,
        far_e,
        far_o,
        end_e,
        end_o,
        edge_e,
        edge_o,
        *parts,
        out_specs=[ANYWHERE, ANYWHERE],
        scratch=[
            pltpu.VMEM((SLICES, ROWS, width), F32),
            pltpu.VMEM((ROWS, chunk), F32),
            pltpu.VMEM((2, 8, width), F32),
            pltpu.SemaphoreType.DMA((1 + tiles // min(4, tiles) * SLICES,)),
        ],
    )


def solution(mesh):
    counts = (mesh.shape["tm"], mesh.shape["lat"])
    return jax.shard_map(
        functools.partial(body, counts),
        mesh=mesh,
        in_specs=(P("tm", "lat", None), P(None, "tm", "lat", None), P("lat", "tm")),
        out_specs=(P("tm", "lat", None), P("lat", "tm")),
        check_vma=False,
    )
```

```python
import functools
import math

import jax
import jax.numpy as jnp
from jax import lax
from jax.experimental import pallas as pl
from jax.experimental.pallas import tpu as pltpu
from jax.sharding import PartitionSpec as P

F32 = jnp.float32
LANES = 128
SLICES = 4
ROWS = 16
HELD = 24


def step_weights():
    centre_value = 6.525
    spread_value = 6.475
    root_order = (3, 0, 2, 1)
    return [
        1.0 / (centre_value + spread_value * math.cos(math.pi * (2 * section + 1) / 8.0))
        for section in root_order
    ]


W0, W1, W2, W3 = step_weights()
SUM2 = W2 + W3
PROD2 = W2 * W3
COEFFS = (
    W0 + W1 + W2 + W3,
    W0 * (W1 + W2 + W3) + W1 * SUM2 + W2 * W3,
    W0 * (W1 * W2 + W1 * W3 + W2 * W3) + W1 * PROD2,
    W0 * W1 * W2 * W3,
)


def even_pairs(count):
    return [(i, i ^ 1) for i in range(count)]


def odd_pairs(count):
    return [(i, (i + 1) % count if i % 2 else (i - 1) % count) for i in range(count)]


def lat_odd_pairs(tm_count, lat_count):
    ring = {0: 1, 1: 3, 3: 2, 2: 0} if tm_count == 4 else dict(even_pairs(tm_count))
    pairs = []
    for t in range(tm_count):
        for l, (_, other) in enumerate(odd_pairs(lat_count)):
            end = l in (0, lat_count - 1)
            pairs.append((t * lat_count + l, ring[t] * lat_count + l if end else t * lat_count + other))
    return pairs


def inner_odd_pairs(tm_count, lat_count):
    pairs = []
    for t, (_, other) in enumerate(odd_pairs(tm_count)):
        for l in range(lat_count):
            end = t in (0, tm_count - 1)
            pairs.append((t * lat_count + l, t * lat_count + (l ^ 1) if end else other * lat_count + l))
    return pairs


def shape_of(*dims):
    return jax.ShapeDtypeStruct(dims, F32)


IN_PLACE = pl.BlockSpec(memory_space=pltpu.VMEM)
ANYWHERE = pl.BlockSpec(memory_space=pltpu.HBM)


def call(kernel, outs, *args, in_specs=None, out_specs=None, scratch=(), aliases=None, cost=0):
    many = isinstance(outs, (list, tuple))
    return pl.pallas_call(
        kernel,
        out_shape=outs,
        in_specs=in_specs or [IN_PLACE] * len(args),
        out_specs=out_specs or ([IN_PLACE] * len(outs) if many else IN_PLACE),
        scratch_shapes=scratch,
        input_output_aliases=aliases or {},
        cost_estimate=pl.CostEstimate(flops=cost, bytes_accessed=cost, transcendentals=0),
        compiler_params=pltpu.CompilerParams(vmem_limit_bytes=12 << 20),
    )(*args)


def tile_at(tile):
    return pl.ds(pl.multiple_of(tile * LANES, LANES), LANES)


def each_tile(width, work, unroll=8):
    def step(tile, carry):
        work(tile, tile_at(tile))
        return carry

    tiles = width // LANES
    lax.fori_loop(0, tiles, step, 0, unroll=min(unroll, tiles))


def iota(rows, dim):
    return lax.broadcasted_iota(jnp.int32, (rows, LANES), dim)


def down(cells, by):
    return pltpu.roll(cells, by, 0)


def around(ref, index, tile, tiles, circular=True):
    cells = ref[index, :, tile_at(tile)]
    before = ref[index, :, tile_at(lax.rem(tile + tiles - 1, tiles))]
    after = ref[index, :, tile_at(lax.rem(tile + 1, tiles))]
    lane = iota(cells.shape[0], 1)
    west = pltpu.roll(jnp.where(lane == LANES - 1, before, cells), 1, 1)
    east = pltpu.roll(jnp.where(lane == 0, after, cells), LANES - 1, 1)
    return cells, west + east + (down(cells, 1) + down(cells, cells.shape[0] - 1))


def places(tm_count):
    t = lax.axis_index("tm")
    odd = lax.rem(t, 2)
    return odd, jnp.where(odd == 1, t < tm_count - 1, t > 0).astype(F32)


def lat_places(lat_count):
    l = lax.axis_index("lat")
    return lax.rem(l, 2) == 0, (l < lat_count - 1).astype(F32), (l > 0).astype(F32)


def mirrored(odd, j):
    return jnp.where(odd == 1, SLICES - 1 - j, j)


def corner_rows(blocks):
    return 8 * (blocks // 2)


def corner_kernel(s0, s1, s2, s3, rng, even_out, odd_out, held, even_two, odd_two):
    held[...] = rng[...]
    for out, cells in ((even_two, (s3, s2)), (odd_two, (s0, s1))):
        for i in range(2):
            out[i * ROWS : (i + 1) * ROWS] = cells[i][...]
    chunk = rng.shape[1]
    per = chunk // LANES
    half = s0.shape[1] // 2
    sub = iota(8, 0)
    for cells, out in ((s3, even_out), (s0, odd_out)):
        out[:ROWS] = rng[...]
        for tile in range(half // LANES):
            left, right = (
                jnp.where(sub < 4, cells[:8, cols], cells[ROWS - 8 :, cols])
                for cols in (pl.ds(at + tile * LANES, LANES) for at in (0, half))
            )
            at = ROWS + tile // per * 8
            inner = (sub >= 2) & (sub < 6)
            out[at : at + 8, tile % per * LANES : (tile % per + 1) * LANES] = jnp.where(inner, down(right, 4), left)


def corners(message, tile, tiles):
    half, per = tiles // 2, message.shape[1] // LANES
    place = lax.rem(tile, half)
    at = pl.multiple_of(ROWS + lax.div(place, per) * 8, 8)
    rows = message[pl.ds(at, 8), tile_at(lax.rem(place, per))]
    return jnp.where(tile < half, rows, down(rows, 4))


def rows_kernel(forward, *refs):
    slabs, (near_e, near_o), refs = refs[:SLICES], refs[SLICES : SLICES + 2], refs[SLICES + 2 :]
    tiles = slabs[0].shape[1] // LANES
    even_lat, _, _ = lat_places(2)
    *field, full, la, lb = refs
    if forward:
        t = lax.axis_index("tm")
        chunk = field[0].shape[1]
        for i, piece in enumerate((field[0], near_e, field[1], near_o)):
            full[:, pl.ds(pl.multiple_of((t ^ i) * chunk, chunk), chunk)] = piece[:ROWS]
    else:
        full[...] = field[0][...]
    sub = iota(8, 0)

    def work(tile, cols):
        for i in range(SLICES // 2):
            one, two, field = slabs[2 * i], slabs[2 * i + 1], full
            first = jnp.where(sub == 3, down(field[:8, cols], 3 - i), down(two[:8, cols], 5))
            first = jnp.where(sub < 3, one[:8, cols], first)
            last = jnp.where(sub == 4, down(field[8:, cols], 6 - i), down(two[8:, cols], 3))
            last = jnp.where(sub > 4, one[8:, cols], last)
            la[8 * i : 8 * i + 8, cols] = jnp.where(even_lat, last, first)
            lb[8 * i : 8 * i + 8, cols] = jnp.where(even_lat, first, last)
        from_e, from_o = (corners(ref, tile, tiles) for ref in (near_e, near_o))
        first = jnp.where(sub < 2, from_e, down(from_o, 2))
        last = jnp.where(sub >= 6, from_e, down(from_o, 6))
        la[16:, cols] = jnp.where(even_lat, last, first)
        lb[16:, cols] = jnp.where(even_lat, first, last)

    each_tile(full.shape[1], work)


def below_above(lat_count, la, lb, at, cols):
    even_lat, has_below, has_above = lat_places(lat_count)
    a, b = la[pl.ds(at, 8), cols], lb[pl.ds(at, 8), cols]
    return jnp.where(even_lat, a, b) * has_below, jnp.where(even_lat, b, a) * has_above


def joined(cells, below, above):
    return jnp.concatenate([cells, jnp.where(iota(8, 0) < 4, below, above)], axis=0)


def lat_mask(lat_count):
    _, has_below, has_above = lat_places(lat_count)
    row = iota(HELD, 0)
    return jnp.where(row < ROWS, 1.0, jnp.where(row < ROWS + 4, has_below, has_above))


def at(cells, j):
    return cells[j] if 0 <= j < SLICES else 0.0


def own_kernel(counts, s0, s1, s2, s3, full, la, lb, by0, by1, by2, grad, noise, rr, edge_e, edge_o, u, y1, y2, end_e, end_o):
    tm_count, lat_count = counts
    K0, K1, K2, _ = COEFFS
    odd, has_before = places(tm_count)
    width = full.shape[1]
    tiles = width // LANES
    mask = lat_mask(lat_count)
    back = 1.0 + has_before

    end_e[...] = s1[...]
    end_o[...] = s2[...]

    def gather(tile, cols):
        first, last = below_above(lat_count, la, lb, 0, cols)
        second, ahead = below_above(lat_count, la, lb, 8, cols)
        u[0, :, cols] = joined(s0[:, cols], first, last)
        u[1, :, cols] = joined(s1[:, cols], down(first, 3), down(last, 5))
        u[2, :, cols] = joined(s2[:, cols], second, ahead)
        u[3, :, cols] = joined(s3[:, cols], down(second, 3), down(ahead, 5))
        sub = iota(8, 0)
        below = jnp.where(sub == 0, down(first, 5), down(second, 6))
        above = jnp.where(sub == 7, down(ahead, 3), down(last, 2))
        rr[:, cols] = joined(full[:, cols], below, above) + 6.0

    each_tile(width, gather)

    def once(tile, cols):
        field = rr[:, cols]
        for j in range(SLICES):
            cells, beside = around(u, j, tile, tiles)
            y1[j, :, cols] = (beside - field * cells) * mask

    each_tile(width, once)

    def twice(tile, cols):
        field = rr[:, cols]
        c0 = [u[j, :ROWS, cols] for j in range(SLICES)]
        c1 = [y1[j, :ROWS, cols] for j in range(SLICES)]
        total = jnp.zeros((ROWS, LANES), F32)
        for j in range(SLICES):
            cells, beside = around(y1, j, tile, tiles)
            c2 = (beside - field * cells) * mask
            y2[j, :, cols] = c2
            one = c1[j] + (at(c0, j - 1) + at(c0, j + 1))
            two = c2[:ROWS] + 2.0 * (at(c1, j - 1) + at(c1, j + 1))
            two = two + (back if j == 0 else 2.0) * c0[j] + (at(c0, j - 2) + at(c0, j + 2))
            place = pl.ds(mirrored(odd, j), 1)
            total = total + c0[j] * by0[place, :, cols][0] + one * by1[place, :, cols][0] + two * by2[place, :, cols][0]
            noise[j, :, cols] = K0 * c0[j] + K1 * one + K2 * two
        grad[:, cols] = -total

    each_tile(width, twice)
    chunk = edge_e.shape[1]
    blocks = width // chunk
    sub = iota(8, 0)
    for out, start, shifts in ((edge_o, 0, (3, 5)), (edge_e, 8, (0, 0))):
        for tile in range(chunk // LANES):
            for v in range(0, edge_rows(blocks), 8):
                rows = jnp.zeros((8, LANES), F32)
                for k in range(min(4, blocks - v // 2)):
                    cols = pl.ds((v // 2 + k) * chunk + tile * LANES, LANES)
                    below, above = below_above(lat_count, la, lb, start, cols)
                    below = down(below, (shifts[0] + 2 * k + 1) % 8)
                    above = down(above, (shifts[1] + 2 * k + 1) % 8)
                    rows = jnp.where(sub == 2 * k, above, jnp.where(sub == 2 * k + 1, below, rows))
                out[v : v + 8, tile * LANES : (tile + 1) * LANES] = rows


def third_kernel(tm_count, noise, u, y1, y2, rr, _, out):
    _, has_before = places(tm_count)
    width = noise.shape[2]
    tiles = width // LANES
    K3 = COEFFS[3]
    back = 1.0 + has_before

    def thrice(tile, cols):
        field = rr[:ROWS, cols]
        c0 = [u[j, :ROWS, cols] for j in range(SLICES)]
        c1 = [y1[j, :ROWS, cols] for j in range(SLICES)]
        c2 = [y2[j, :ROWS, cols] for j in range(SLICES)]
        for j in range(SLICES):
            cells, beside = around(y2, j, tile, tiles)
            three = beside[:ROWS] - field * cells[:ROWS]
            three = three + 3.0 * (at(c2, j - 1) + at(c2, j + 1) + at(c1, j - 2) + at(c1, j + 2))
            three = three + (3.0 * back if j == 0 else 6.0) * c1[j]
            left, right = (1.0 + back if j == i else 3.0 for i in (1, 0))
            three = three + (left * at(c0, j - 1) + right * at(c0, j + 1) + at(c0, j - 3) + at(c0, j + 3))
            out[j, :, cols] = noise[j, :, cols] + K3 * three

    each_tile(width, thrice)


def edge_rows(blocks):
    return (2 * blocks + 7) // 8 * 8


def near_kernel(counts, forward, grad, near_e, near_o, la, lb, rr, edge_e, edge_o, by1, by2, *refs):
    tm_count, lat_count = counts
    odd, has_before = places(tm_count)
    width = grad.shape[1]
    tiles = width // LANES
    mask = lat_mask(lat_count)
    u, y1 = refs[:2]
    total = refs[-1] if forward else refs[2]

    def gather(tile, cols):
        below, above = below_above(lat_count, la, lb, 16, cols)
        u[0, :, cols] = joined(near_o[:ROWS, cols], down(below, 6), down(above, 2)) * has_before
        u[1, :, cols] = joined(near_e[:ROWS, cols], below, above)

    each_tile(width, gather)

    def once(tile, cols):
        field = rr[:, cols]
        out = grad[:, cols]
        for i, two in enumerate((near_o, near_e)):
            cells, beside = around(u, i, tile, tiles)
            c1 = (beside - field * cells) * mask
            y1[i, :, cols] = c1
            beyond = two[ROWS:, cols] * has_before if i == 0 else two[ROWS:, cols]
            j, inner = (0, 1) if i == 0 else (SLICES - 1, SLICES - 2)
            j, inner = pl.ds(mirrored(odd, j), 1), pl.ds(mirrored(odd, inner), 1)
            add = cells[:ROWS] * (by1[j, :, cols][0] + by2[inner, :, cols][0])
            out = out - (add + (2.0 * c1[:ROWS] + beyond) * by2[j, :, cols][0])
        total[:, cols] = out

    each_tile(width, once, unroll=2)
    if forward:
        t = lax.axis_index("tm")
        chunk = refs[2].shape[1]
        for i, out in enumerate(refs[2:6]):
            out[:ROWS] = total[:, pl.ds(pl.multiple_of((t ^ i) * chunk, chunk), chunk)]
        refs[3][ROWS:] = edge_e[...]
        refs[5][ROWS:] = edge_o[...]
def last_kernel(tm_count, own, u, y1, rr, near_e, near_o, end_e, end_o, edge_e, edge_o, *refs):
    *parts, noise, gradient, out, total, beside_far, sems = refs
    odd, has_before = places(tm_count)
    width = own.shape[2]
    tiles = width // LANES
    K0, K1, K2, K3 = COEFFS
    chunk = total.shape[1]
    for i, more in enumerate(parts):
        total[...] = more[:ROWS] if i == 0 else total[...] + more[:ROWS]
    copies = [pltpu.make_async_copy(total, gradient, sems.at[0])]
    copies[0].start()
    blocks = width // chunk
    start = edge_e.shape[0] - edge_rows(blocks)
    sub = iota(8, 0)
    for i, ref in enumerate((edge_o, edge_e)):
        for b in range(blocks):
            for tile in range(chunk // LANES):
                k, at = b % 4, start + b // 4 * 8
                rows = ref[at : at + 8, tile * LANES : (tile + 1) * LANES]
                rows = jnp.where(sub < 4, down(rows, (8 - 2 * k) % 8), down(rows, 6 - 2 * k))
                beside_far[i, :, b * chunk + tile * LANES : b * chunk + (tile + 1) * LANES] = rows
    row, lane = iota(ROWS, 0), iota(ROWS, 1)

    def work(tile, cols):
        field = rr[:ROWS, cols]
        result = [own[j, :, cols] for j in range(SLICES)]
        for i, (far, end) in enumerate(((near_o, end_o), (near_e, end_e))):
            cells, beside = around(y1, i, tile, tiles)
            n0, n1 = u[i, :ROWS, cols], cells[:ROWS]
            n2 = beside[:ROWS] - field * n1
            f0 = far[ROWS:, cols]
            before = far[ROWS:, tile_at(lax.rem(tile + tiles - 1, tiles))]
            after = far[ROWS:, tile_at(lax.rem(tile + 1, tiles))]
            west = pltpu.roll(jnp.where(lane == LANES - 1, before, f0), 1, 1)
            east = pltpu.roll(jnp.where(lane == 0, after, f0), LANES - 1, 1)
            edge = jnp.concatenate([beside_far[i, :, cols]] * 2, axis=0)
            above = jnp.where(row == 0, edge, down(f0, 1))
            below = jnp.where(row == ROWS - 1, edge, down(f0, ROWS - 1))
            f1 = west + east + (above + below) - field * f0
            beyond = 3.0 * f1 + end[:, cols]
            if i == 0:
                f0, beyond = f0 * has_before, beyond * has_before
            a, b, c = (0, 1, 2) if i == 0 else (3, 2, 1)
            result[a] = result[a] + (K1 + 3.0 * K3) * n0 + K2 * (2.0 * n1 + f0) + K3 * (3.0 * n2 + beyond)
            result[b] = result[b] + K2 * n0 + K3 * (3.0 * n1 + f0)
            result[c] = result[c] + K3 * n0
        for j in range(SLICES):
            out[j, :, cols] = result[j]

    per = min(4, tiles)
    for q in range(0, tiles, per):

        def step(tile, carry):
            work(tile, tile_at(tile))
            return carry

        lax.fori_loop(q, q + per, step, 0, unroll=per)
        cols = pl.ds(q * LANES, per * LANES)
        for j in range(SLICES):
            copy = pltpu.make_async_copy(
                out.at[j, :, cols], noise.at[mirrored(odd, j), :, cols], sems.at[1 + q // per * SLICES + j]
            )
            copy.start()
            copies.append(copy)
    for copy in copies:
        copy.wait()


def body(counts, cotangent, iterates, range_field):
    tm_count, lat_count = counts
    forward = tm_count == 4
    slices, rows, width = cotangent.shape
    chunk = range_field.shape[1]
    assert slices == SLICES and rows == ROWS
    even, odd = even_pairs(tm_count), odd_pairs(tm_count)
    lat_even, lat_odd = even_pairs(lat_count), lat_odd_pairs(tm_count, lat_count)
    inner = inner_odd_pairs(tm_count, lat_count)
    y_pairs = [(i, i ^ 2) for i in range(tm_count)]
    one = shape_of(ROWS, width)
    extra = edge_rows(width // chunk)

    flip = lax.rem(lax.axis_index("tm"), 2) == 1
    slabs = [
        lax.dynamic_index_in_dim(cotangent, jnp.where(flip, SLICES - 1 - j, j), 0, False) for j in range(SLICES)
    ]
    message = shape_of(ROWS + corner_rows(width // chunk), chunk)
    two = shape_of(2 * ROWS, width)
    corner_e, corner_o, held, near_e, near_o = call(
        corner_kernel, [message, message, shape_of(ROWS, chunk), two, two], *slabs, range_field
    )
    corner_e, corner_o = lax.ppermute(corner_e, "tm", even), lax.ppermute(corner_o, "tm", odd)
    if forward:
        field = [held, lax.ppermute(range_field, "tm", y_pairs)]
    else:
        field = [lax.all_gather(range_field, "tm", axis=1, tiled=True)]
    near_e, near_o = lax.ppermute(near_e, "tm", even), lax.ppermute(near_o, ("tm", "lat"), inner)
    x1, x2, x3 = iterates[0], iterates[1], iterates[2]
    scales = (W3 * x3 + W2 * x2 + W1 * x1, (W2 * W3) * x2 + (W1 * SUM2) * x1, (W1 * PROD2) * x1)
    pair = shape_of(24, width)
    full, la1, lb1 = call(functools.partial(rows_kernel, forward), [one, pair, pair], *slabs, corner_e, corner_o, *field)
    la1, lb1 = lax.ppermute(la1, "lat", lat_even), lax.ppermute(lb1, ("tm", "lat"), lat_odd)
    deep = shape_of(SLICES, HELD, width)
    own = shape_of(SLICES, ROWS, width)
    edge = shape_of(extra, chunk)
    grad, own, rr, edge_e, edge_o, *powers, end_e, end_o = call(
        functools.partial(own_kernel, counts),
        [one, own, shape_of(HELD, width), edge, edge, deep, deep, deep, one, one],
        *slabs,
        full,
        la1,
        lb1,
        *scales,
    )
    end_e, end_o = lax.ppermute(end_e, "tm", even), lax.ppermute(end_o, ("tm", "lat"), inner)
    pair = shape_of(2, HELD, width)
    if forward:
        outs = [shape_of(ROWS + more, chunk) for more in (0, extra, 0, extra)]
    else:
        outs = [one]
    u, y1, *outs = call(
        functools.partial(near_kernel, counts, forward),
        [pair, pair] + outs,
        grad,
        near_e,
        near_o,
        la1,
        lb1,
        rr,
        edge_e,
        edge_o,
        *scales[1:],
        scratch=[pltpu.VMEM((ROWS, width), F32)] if forward else (),
    )
    own = call(
        functools.partial(third_kernel, tm_count), shape_of(SLICES, ROWS, width), own, *powers, rr, u
    )
    if forward:
        g1, g2, g3 = (lax.ppermute(g, "tm", p) for g, p in zip(outs[1:], (even, y_pairs, odd)))
        edge_e, edge_o = g1, g3
        parts = (outs[0], g1, g2, g3)
    else:
        parts = (lax.psum_scatter(outs[0], "tm", scatter_dimension=1, tiled=True),)
        edge_e, edge_o = lax.ppermute(edge_e, "tm", even), lax.ppermute(edge_o, "tm", odd)
    tiles = width // LANES
    return call(
        functools.partial(last_kernel, tm_count),
        [shape_of(SLICES, ROWS, width), shape_of(ROWS, chunk)],
        own,
        u,
        y1,
        rr,
        near_e,
        near_o,
        end_e,
        end_o,
        edge_e,
        edge_o,
        *parts,
        out_specs=[ANYWHERE, ANYWHERE],
        scratch=[
            pltpu.VMEM((SLICES, ROWS, width), F32),
            pltpu.VMEM((ROWS, chunk), F32),
            pltpu.VMEM((2, 8, width), F32),
            pltpu.SemaphoreType.DMA((1 + tiles // min(4, tiles) * SLICES,)),
        ],
    )


def solution(mesh):
    counts = (mesh.shape["tm"], mesh.shape["lat"])
    return jax.shard_map(
        functools.partial(body, counts),
        mesh=mesh,
        in_specs=(P("tm", "lat", None), P(None, "tm", "lat", None), P("lat", "tm")),
        out_specs=(P("tm", "lat", None), P("lat", "tm")),
        check_vma=False,
    )
```

```python
import functools
import math

import jax
import jax.numpy as jnp
from jax import lax
from jax.experimental import pallas as pl
from jax.experimental.pallas import tpu as pltpu
from jax.sharding import PartitionSpec as P

F32 = jnp.float32
LANES = 128
SLICES = 4
ROWS = 16
HELD = 24


def step_weights():
    centre_value = 6.525
    spread_value = 6.475
    root_order = (3, 0, 2, 1)
    return [
        1.0 / (centre_value + spread_value * math.cos(math.pi * (2 * section + 1) / 8.0))
        for section in root_order
    ]


W0, W1, W2, W3 = step_weights()
SUM2 = W2 + W3
PROD2 = W2 * W3
COEFFS = (
    W0 + W1 + W2 + W3,
    W0 * (W1 + W2 + W3) + W1 * SUM2 + W2 * W3,
    W0 * (W1 * W2 + W1 * W3 + W2 * W3) + W1 * PROD2,
    W0 * W1 * W2 * W3,
)


def even_pairs(count):
    return [(i, i ^ 1) for i in range(count)]


def odd_pairs(count):
    return [(i, (i + 1) % count if i % 2 else (i - 1) % count) for i in range(count)]


def lat_odd_pairs(tm_count, lat_count):
    ring = {0: 1, 1: 3, 3: 2, 2: 0} if tm_count == 4 else dict(even_pairs(tm_count))
    pairs = []
    for t in range(tm_count):
        for l, (_, other) in enumerate(odd_pairs(lat_count)):
            end = l in (0, lat_count - 1)
            pairs.append((t * lat_count + l, ring[t] * lat_count + l if end else t * lat_count + other))
    return pairs


def inner_odd_pairs(tm_count, lat_count):
    pairs = []
    for t, (_, other) in enumerate(odd_pairs(tm_count)):
        for l in range(lat_count):
            end = t in (0, tm_count - 1)
            pairs.append((t * lat_count + l, t * lat_count + (l ^ 1) if end else other * lat_count + l))
    return pairs


def shape_of(*dims):
    return jax.ShapeDtypeStruct(dims, F32)


IN_PLACE = pl.BlockSpec(memory_space=pltpu.VMEM)
ANYWHERE = pl.BlockSpec(memory_space=pltpu.HBM)


def call(kernel, outs, *args, in_specs=None, out_specs=None, scratch=(), aliases=None, cost=0):
    many = isinstance(outs, (list, tuple))
    return pl.pallas_call(
        kernel,
        out_shape=outs,
        in_specs=in_specs or [IN_PLACE] * len(args),
        out_specs=out_specs or ([IN_PLACE] * len(outs) if many else IN_PLACE),
        scratch_shapes=scratch,
        input_output_aliases=aliases or {},
        cost_estimate=pl.CostEstimate(flops=cost, bytes_accessed=cost, transcendentals=0),
        compiler_params=pltpu.CompilerParams(vmem_limit_bytes=12 << 20),
    )(*args)


def tile_at(tile):
    return pl.ds(pl.multiple_of(tile * LANES, LANES), LANES)


def each_tile(width, work, unroll=16):
    def step(tile, carry):
        work(tile, tile_at(tile))
        return carry

    tiles = width // LANES
    lax.fori_loop(0, tiles, step, 0, unroll=min(unroll, tiles))


def iota(rows, dim):
    return lax.broadcasted_iota(jnp.int32, (rows, LANES), dim)


def down(cells, by):
    return pltpu.roll(cells, by, 0)


def around(ref, index, tile, tiles, circular=True):
    cells = ref[index, :, tile_at(tile)]
    before = ref[index, :, tile_at(lax.rem(tile + tiles - 1, tiles))]
    after = ref[index, :, tile_at(lax.rem(tile + 1, tiles))]
    lane = iota(cells.shape[0], 1)
    west = pltpu.roll(jnp.where(lane == LANES - 1, before, cells), 1, 1)
    east = pltpu.roll(jnp.where(lane == 0, after, cells), LANES - 1, 1)
    return cells, west + east + (down(cells, 1) + down(cells, cells.shape[0] - 1))


def places(tm_count):
    t = lax.axis_index("tm")
    odd = lax.rem(t, 2)
    return odd, jnp.where(odd == 1, t < tm_count - 1, t > 0).astype(F32)


def lat_places(lat_count):
    l = lax.axis_index("lat")
    return lax.rem(l, 2) == 0, (l < lat_count - 1).astype(F32), (l > 0).astype(F32)


def mirrored(odd, j):
    return jnp.where(odd == 1, SLICES - 1 - j, j)


def corner_rows(blocks):
    return 8 * (blocks // 2)


def corner_kernel(s0, s1, s2, s3, rng, even_out, odd_out, held, even_two, odd_two):
    held[...] = rng[...]
    for out, cells in ((even_two, (s3, s2)), (odd_two, (s0, s1))):
        for i in range(2):
            out[i * ROWS : (i + 1) * ROWS] = cells[i][...]
    chunk = rng.shape[1]
    per = chunk // LANES
    half = s0.shape[1] // 2
    sub = iota(8, 0)
    for cells, out in ((s3, even_out), (s0, odd_out)):
        out[:ROWS] = rng[...]
        for tile in range(half // LANES):
            left, right = (
                jnp.where(sub < 4, cells[:8, cols], cells[ROWS - 8 :, cols])
                for cols in (pl.ds(at + tile * LANES, LANES) for at in (0, half))
            )
            at = ROWS + tile // per * 8
            inner = (sub >= 2) & (sub < 6)
            out[at : at + 8, tile % per * LANES : (tile % per + 1) * LANES] = jnp.where(inner, down(right, 4), left)


def corners(message, tile, tiles):
    half, per = tiles // 2, message.shape[1] // LANES
    place = lax.rem(tile, half)
    at = pl.multiple_of(ROWS + lax.div(place, per) * 8, 8)
    rows = message[pl.ds(at, 8), tile_at(lax.rem(place, per))]
    return jnp.where(tile < half, rows, down(rows, 4))


def rows_kernel(forward, *refs):
    slabs, (near_e, near_o), refs = refs[:SLICES], refs[SLICES : SLICES + 2], refs[SLICES + 2 :]
    tiles = slabs[0].shape[1] // LANES
    even_lat, _, _ = lat_places(2)
    *field, full, la, lb = refs
    if forward:
        t = lax.axis_index("tm")
        chunk = field[0].shape[1]
        for i, piece in enumerate((field[0], near_e, field[1], near_o)):
            full[:, pl.ds(pl.multiple_of((t ^ i) * chunk, chunk), chunk)] = piece[:ROWS]
    else:
        full[...] = field[0][...]
    sub = iota(8, 0)

    def work(tile, cols):
        for i in range(SLICES // 2):
            one, two, field = slabs[2 * i], slabs[2 * i + 1], full
            first = jnp.where(sub == 3, down(field[:8, cols], 3 - i), down(two[:8, cols], 5))
            first = jnp.where(sub < 3, one[:8, cols], first)
            last = jnp.where(sub == 4, down(field[8:, cols], 6 - i), down(two[8:, cols], 3))
            last = jnp.where(sub > 4, one[8:, cols], last)
            la[8 * i : 8 * i + 8, cols] = jnp.where(even_lat, last, first)
            lb[8 * i : 8 * i + 8, cols] = jnp.where(even_lat, first, last)
        from_e, from_o = (corners(ref, tile, tiles) for ref in (near_e, near_o))
        first = jnp.where(sub < 2, from_e, down(from_o, 2))
        last = jnp.where(sub >= 6, from_e, down(from_o, 6))
        la[16:, cols] = jnp.where(even_lat, last, first)
        lb[16:, cols] = jnp.where(even_lat, first, last)

    each_tile(full.shape[1], work)


def below_above(lat_count, la, lb, at, cols):
    even_lat, has_below, has_above = lat_places(lat_count)
    a, b = la[pl.ds(at, 8), cols], lb[pl.ds(at, 8), cols]
    return jnp.where(even_lat, a, b) * has_below, jnp.where(even_lat, b, a) * has_above


def joined(cells, below, above):
    return jnp.concatenate([cells, jnp.where(iota(8, 0) < 4, below, above)], axis=0)


def lat_mask(lat_count):
    _, has_below, has_above = lat_places(lat_count)
    row = iota(HELD, 0)
    return jnp.where(row < ROWS, 1.0, jnp.where(row < ROWS + 4, has_below, has_above))


def at(cells, j):
    return cells[j] if 0 <= j < SLICES else 0.0


def own_kernel(counts, s0, s1, s2, s3, full, la, lb, by0, by1, by2, grad, noise, rr, u, y1, y2, end_e, other):
    tm_count, lat_count = counts
    K0, K1, K2, _ = COEFFS
    odd, has_before = places(tm_count)
    width = full.shape[1]
    tiles = width // LANES
    mask = lat_mask(lat_count)
    back = 1.0 + has_before

    tm_four = tm_count == 4

    def gather(tile, cols):
        first, last = below_above(lat_count, la, lb, 0, cols)
        second, ahead = below_above(lat_count, la, lb, 8, cols)
        u[0, :, cols] = joined(s0[:, cols], first, last)
        u[1, :, cols] = joined(s1[:, cols], down(first, 3), down(last, 5))
        u[2, :, cols] = joined(s2[:, cols], second, ahead)
        u[3, :, cols] = joined(s3[:, cols], down(second, 3), down(ahead, 5))
        sub = iota(8, 0)
        end_e[:8, cols] = s1[:8, cols] + jnp.where(sub == 0, 3.0 * down(ahead, 1), 0.0)
        end_e[8:, cols] = s1[8:, cols] + jnp.where(sub == 7, 3.0 * down(second, 7), 0.0)
        if not tm_four:
            other[:8, cols] = s2[:8, cols] + jnp.where(sub == 0, 3.0 * down(last, 6), 0.0)
            other[8:, cols] = s2[8:, cols] + jnp.where(sub == 7, 3.0 * down(first, 2), 0.0)
        below = jnp.where(sub == 0, down(first, 5), down(second, 6))
        above = jnp.where(sub == 7, down(ahead, 3), down(last, 2))
        rr[:, cols] = joined(full[:, cols], below, above) + 6.0

    each_tile(width, gather)

    def once(tile, cols):
        field = rr[:, cols]
        for j in range(SLICES):
            cells, beside = around(u, j, tile, tiles)
            y1[j, :, cols] = (beside - field * cells) * mask

    each_tile(width, once)

    def twice(tile, cols):
        field = rr[:, cols]
        c0 = [u[j, :ROWS, cols] for j in range(SLICES)]
        c1 = [y1[j, :ROWS, cols] for j in range(SLICES)]
        total = jnp.zeros((ROWS, LANES), F32)
        for j in range(SLICES):
            cells, beside = around(y1, j, tile, tiles)
            c2 = (beside - field * cells) * mask
            y2[j, :, cols] = c2
            one = c1[j] + (at(c0, j - 1) + at(c0, j + 1))
            two = c2[:ROWS] + 2.0 * (at(c1, j - 1) + at(c1, j + 1))
            two = two + (back if j == 0 else 2.0) * c0[j] + (at(c0, j - 2) + at(c0, j + 2))
            place = pl.ds(mirrored(odd, j), 1)
            total = total + c0[j] * by0[place, :, cols][0] + one * by1[place, :, cols][0] + two * by2[place, :, cols][0]
            noise[j, :, cols] = K0 * c0[j] + K1 * one + K2 * two
        grad[:, cols] = -total

    each_tile(width, twice)
    if not tm_four:
        return
    chunk = other.shape[1]
    blocks = width // chunk
    sub = iota(8, 0)
    for tile in range(chunk // LANES):
        for v in range(0, edge_rows(blocks), 8):
            rows = jnp.zeros((8, LANES), F32)
            for k in range(min(4, blocks - v // 2)):
                cols = pl.ds((v // 2 + k) * chunk + tile * LANES, LANES)
                below, above = below_above(lat_count, la, lb, 0, cols)
                below, above = down(below, (2 * k + 4) % 8), down(above, (2 * k + 6) % 8)
                rows = jnp.where(sub == 2 * k, above, jnp.where(sub == 2 * k + 1, below, rows))
            other[v : v + 8, tile * LANES : (tile + 1) * LANES] = rows


def edge_rows(blocks):
    return (2 * blocks + 7) // 8 * 8


def near_kernel(counts, forward, grad, near_e, near_o, la, lb, rr, edge_o, by1, by2, *refs):
    tm_count, lat_count = counts
    odd, has_before = places(tm_count)
    width = grad.shape[1]
    tiles = width // LANES
    mask = lat_mask(lat_count)
    u, y1 = refs[:2]
    total = refs[-1] if forward else refs[2]

    def gather(tile, cols):
        below, above = below_above(lat_count, la, lb, 16, cols)
        u[0, :, cols] = joined(near_o[:ROWS, cols], down(below, 6), down(above, 2)) * has_before
        u[1, :, cols] = joined(near_e[:ROWS, cols], below, above)

    each_tile(width, gather)

    def once(tile, cols):
        field = rr[:, cols]
        out = grad[:, cols]
        for i, two in enumerate((near_o, near_e)):
            cells, beside = around(u, i, tile, tiles)
            c1 = (beside - field * cells) * mask
            y1[i, :, cols] = c1
            beyond = two[ROWS:, cols] * has_before if i == 0 else two[ROWS:, cols]
            j, inner = (0, 1) if i == 0 else (SLICES - 1, SLICES - 2)
            j, inner = pl.ds(mirrored(odd, j), 1), pl.ds(mirrored(odd, inner), 1)
            add = cells[:ROWS] * (by1[j, :, cols][0] + by2[inner, :, cols][0])
            out = out - (add + (2.0 * c1[:ROWS] + beyond) * by2[j, :, cols][0])
        total[:, cols] = out

    each_tile(width, once)
    if forward:
        t = lax.axis_index("tm")
        chunk = refs[2].shape[1]
        for i, out in enumerate(refs[2:6]):
            out[:ROWS] = total[:, pl.ds(pl.multiple_of((t ^ i) * chunk, chunk), chunk)]
        refs[5][ROWS:] = edge_o[...]
def noise_kernel(tm_count, own, p0, p1, p2, u, y1, rr, near_e, near_o, end_e, end_o, noise, first, out, sems):
    odd, has_before = places(tm_count)
    width = own.shape[2]
    tiles = width // LANES
    _, K1, K2, K3 = COEFFS
    back = 1.0 + has_before
    row, lane = iota(ROWS, 0), iota(ROWS, 1)

    def work(tile, cols):
        field = rr[:ROWS, cols]
        c0, c1, c2 = ([ref[j, :ROWS, cols] for j in range(SLICES)] for ref in (p0, p1, p2))
        result = []
        for j in range(SLICES):
            cells, beside = around(p2, j, tile, tiles)
            three = beside[:ROWS] - field * cells[:ROWS]
            three = three + 3.0 * (at(c2, j - 1) + at(c2, j + 1) + at(c1, j - 2) + at(c1, j + 2))
            three = three + (3.0 * back if j == 0 else 6.0) * c1[j]
            left, right = (1.0 + back if j == i else 3.0 for i in (1, 0))
            three = three + (left * at(c0, j - 1) + right * at(c0, j + 1) + at(c0, j - 3) + at(c0, j + 3))
            result.append(own[j, :, cols] + K3 * three)
        for i, (far, end) in enumerate(((near_o, end_o), (near_e, end_e))):
            cells, beside = around(y1, i, tile, tiles)
            n0, n1 = u[i, :ROWS, cols], cells[:ROWS]
            n2 = beside[:ROWS] - field * n1
            f0 = far[ROWS:, cols]
            before = far[ROWS:, tile_at(lax.rem(tile + tiles - 1, tiles))]
            after = far[ROWS:, tile_at(lax.rem(tile + 1, tiles))]
            west = pltpu.roll(jnp.where(lane == LANES - 1, before, f0), 1, 1)
            east = pltpu.roll(jnp.where(lane == 0, after, f0), LANES - 1, 1)
            above = jnp.where(row == 0, 0.0, down(f0, 1))
            below = jnp.where(row == ROWS - 1, 0.0, down(f0, ROWS - 1))
            f1 = west + east + (above + below) - field * f0
            beyond = 3.0 * f1 + end[:, cols]
            if i == 0:
                f0, beyond = f0 * has_before, beyond * has_before
            a, b, c = (0, 1, 2) if i == 0 else (3, 2, 1)
            result[a] = result[a] + (K1 + 3.0 * K3) * n0 + K2 * (2.0 * n1 + f0) + K3 * (3.0 * n2 + beyond)
            result[b] = result[b] + K2 * n0 + K3 * (3.0 * n1 + f0)
            result[c] = result[c] + K3 * n0
        first[:, cols] = result[0]
        for j in range(1, SLICES):
            out[j - 1, :, cols] = result[j]

    copies = []
    per = min(4, tiles)
    for q in range(0, tiles, per):

        def step(tile, carry):
            work(tile, tile_at(tile))
            return carry

        lax.fori_loop(q, q + per, step, 0, unroll=per)
        cols = pl.ds(q * LANES, per * LANES)
        for j in range(1, SLICES):
            copy = pltpu.make_async_copy(
                out.at[j - 1, :, cols],
                noise.at[mirrored(odd, j), :, cols],
                sems.at[q // per * (SLICES - 1) + j - 1],
            )
            copy.start()
            copies.append(copy)
    for copy in copies:
        copy.wait()


def last_kernel(tm_count, _, first, *refs):
    *parts, noise, gradient, out, total, sems = refs
    odd, has_before = places(tm_count)
    for i, more in enumerate(parts):
        total[...] = more[:ROWS] if i == 0 else total[...] + more[:ROWS]
    copies = [pltpu.make_async_copy(total, gradient, sems.at[0])]
    copies[0].start()
    chunk = total.shape[1]
    blocks = first.shape[1] // chunk
    scale = 3.0 * COEFFS[3] * has_before
    sub = iota(8, 0)
    if tm_count != 4:
        out[...] = first[...]
    else:
        edges = parts[-1]
        for b in range(blocks):
            for tile in range(chunk // LANES):
                k, at = b % 4, ROWS + b // 4 * 8
                rows = scale * edges[at : at + 8, tile * LANES : (tile + 1) * LANES]
                cols = pl.ds(b * chunk + tile * LANES, LANES)
                out[:8, cols] = first[:8, cols] + jnp.where(sub == 0, down(rows, (8 - 2 * k) % 8), 0.0)
                out[8:, cols] = first[8:, cols] + jnp.where(sub == 7, down(rows, 6 - 2 * k), 0.0)
    copies.append(pltpu.make_async_copy(out, noise.at[mirrored(odd, 0)], sems.at[1]))
    copies[1].start()
    for copy in copies:
        copy.wait()


def body(counts, cotangent, iterates, range_field):
    tm_count, lat_count = counts
    forward = tm_count == 4
    slices, rows, width = cotangent.shape
    chunk = range_field.shape[1]
    assert slices == SLICES and rows == ROWS
    even, odd = even_pairs(tm_count), odd_pairs(tm_count)
    lat_even, lat_odd = even_pairs(lat_count), lat_odd_pairs(tm_count, lat_count)
    inner = inner_odd_pairs(tm_count, lat_count)
    y_pairs = [(i, i ^ 2) for i in range(tm_count)]
    one = shape_of(ROWS, width)
    extra = edge_rows(width // chunk)

    flip = lax.rem(lax.axis_index("tm"), 2) == 1
    slabs = [
        lax.dynamic_index_in_dim(cotangent, jnp.where(flip, SLICES - 1 - j, j), 0, False) for j in range(SLICES)
    ]
    message = shape_of(ROWS + corner_rows(width // chunk), chunk)
    two = shape_of(2 * ROWS, width)
    corner_e, corner_o, held, near_e, near_o = call(
        corner_kernel, [message, message, shape_of(ROWS, chunk), two, two], *slabs, range_field
    )
    corner_e, corner_o = lax.ppermute(corner_e, "tm", even), lax.ppermute(corner_o, "tm", odd)
    if forward:
        field = [held, lax.ppermute(range_field, "tm", y_pairs)]
    else:
        field = [lax.all_gather(range_field, "tm", axis=1, tiled=True)]
    near_e, near_o = lax.ppermute(near_e, "tm", even), lax.ppermute(near_o, ("tm", "lat"), inner)
    x1, x2, x3 = iterates[0], iterates[1], iterates[2]
    scales = (W3 * x3 + W2 * x2 + W1 * x1, (W2 * W3) * x2 + (W1 * SUM2) * x1, (W1 * PROD2) * x1)
    pair = shape_of(24, width)
    full, la1, lb1 = call(functools.partial(rows_kernel, forward), [one, pair, pair], *slabs, corner_e, corner_o, *field)
    la1, lb1 = lax.ppermute(la1, "lat", lat_even), lax.ppermute(lb1, ("tm", "lat"), lat_odd)
    deep = shape_of(SLICES, HELD, width)
    own = shape_of(SLICES, ROWS, width)
    grad, own, rr, *powers, end_e, other = call(
        functools.partial(own_kernel, counts),
        [one, own, shape_of(HELD, width), deep, deep, deep, one, shape_of(extra, chunk) if forward else one],
        *slabs,
        full,
        la1,
        lb1,
        *scales,
    )
    end_e = lax.ppermute(end_e, "tm", even)
    if forward:
        end_o = lax.ppermute(near_e[ROWS:], "tm", y_pairs)
    else:
        end_o = lax.ppermute(other, ("tm", "lat"), inner)
    pair = shape_of(2, HELD, width)
    if forward:
        outs = [shape_of(ROWS + more, chunk) for more in (0, 0, 0, extra)]
    else:
        outs = [one]
    u, y1, *outs = call(
        functools.partial(near_kernel, counts, forward),
        [pair, pair] + outs,
        grad,
        near_e,
        near_o,
        la1,
        lb1,
        rr,
        other,
        *scales[1:],
        scratch=[pltpu.VMEM((ROWS, width), F32)] if forward else (),
    )
    if forward:
        parts = outs[0], *(lax.ppermute(g, "tm", p) for g, p in zip(outs[1:], (even, y_pairs, odd)))
    else:
        parts = (lax.psum_scatter(outs[0], "tm", scatter_dimension=1, tiled=True),)
    quarters = width // LANES // min(4, width // LANES)
    noise, first = call(
        functools.partial(noise_kernel, tm_count),
        [shape_of(SLICES, ROWS, width), one],
        own,
        *powers,
        u,
        y1,
        rr,
        near_e,
        near_o,
        end_e,
        end_o,
        out_specs=[ANYWHERE, IN_PLACE],
        scratch=[
            pltpu.VMEM((SLICES - 1, ROWS, width), F32),
            pltpu.SemaphoreType.DMA((quarters * (SLICES - 1),)),
        ],
    )
    return call(
        functools.partial(last_kernel, tm_count),
        [shape_of(SLICES, ROWS, width), shape_of(ROWS, chunk)],
        noise,
        first,
        *parts,
        in_specs=[ANYWHERE] + [IN_PLACE] * (1 + len(parts)),
        out_specs=[ANYWHERE, ANYWHERE],
        scratch=[pltpu.VMEM((ROWS, width), F32), pltpu.VMEM((ROWS, chunk), F32), pltpu.SemaphoreType.DMA((2,))],
        aliases={0: 0},
    )


def solution(mesh):
    counts = (mesh.shape["tm"], mesh.shape["lat"])
    return jax.shard_map(
        functools.partial(body, counts),
        mesh=mesh,
        in_specs=(P("tm", "lat", None), P(None, "tm", "lat", None), P("lat", "tm")),
        out_specs=(P("tm", "lat", None), P("lat", "tm")),
        check_vma=False,
    )
```

```python
import functools
import math

import jax
import jax.numpy as jnp
from jax import lax
from jax.experimental import pallas as pl
from jax.experimental.pallas import tpu as pltpu
from jax.sharding import PartitionSpec as P

F32 = jnp.float32
LANES = 128
SLICES = 4
ROWS = 16
HELD = 24


def step_weights():
    centre_value = 6.525
    spread_value = 6.475
    root_order = (3, 0, 2, 1)
    return [
        1.0 / (centre_value + spread_value * math.cos(math.pi * (2 * section + 1) / 8.0))
        for section in root_order
    ]


W0, W1, W2, W3 = step_weights()
SUM2 = W2 + W3
PROD2 = W2 * W3
COEFFS = (
    W0 + W1 + W2 + W3,
    W0 * (W1 + W2 + W3) + W1 * SUM2 + W2 * W3,
    W0 * (W1 * W2 + W1 * W3 + W2 * W3) + W1 * PROD2,
    W0 * W1 * W2 * W3,
)


def even_pairs(count):
    return [(i, i ^ 1) for i in range(count)]


def odd_pairs(count):
    return [(i, (i + 1) % count if i % 2 else (i - 1) % count) for i in range(count)]


def lat_odd_pairs(tm_count, lat_count):
    ring = {0: 1, 1: 3, 3: 2, 2: 0} if tm_count == 4 else dict(even_pairs(tm_count))
    pairs = []
    for t in range(tm_count):
        for l, (_, other) in enumerate(odd_pairs(lat_count)):
            end = l in (0, lat_count - 1)
            pairs.append((t * lat_count + l, ring[t] * lat_count + l if end else t * lat_count + other))
    return pairs


def inner_odd_pairs(tm_count, lat_count):
    pairs = []
    for t, (_, other) in enumerate(odd_pairs(tm_count)):
        for l in range(lat_count):
            end = t in (0, tm_count - 1)
            pairs.append((t * lat_count + l, t * lat_count + (l ^ 1) if end else other * lat_count + l))
    return pairs


def shape_of(*dims):
    return jax.ShapeDtypeStruct(dims, F32)


IN_PLACE = pl.BlockSpec(memory_space=pltpu.VMEM)
ANYWHERE = pl.BlockSpec(memory_space=pltpu.HBM)


def call(kernel, outs, *args, in_specs=None, out_specs=None, scratch=(), aliases=None, cost=0):
    many = isinstance(outs, (list, tuple))
    return pl.pallas_call(
        kernel,
        out_shape=outs,
        in_specs=in_specs or [IN_PLACE] * len(args),
        out_specs=out_specs or ([IN_PLACE] * len(outs) if many else IN_PLACE),
        scratch_shapes=scratch,
        input_output_aliases=aliases or {},
        cost_estimate=pl.CostEstimate(flops=cost, bytes_accessed=cost, transcendentals=0),
        compiler_params=pltpu.CompilerParams(vmem_limit_bytes=12 << 20),
    )(*args)


def tile_at(tile):
    return pl.ds(pl.multiple_of(tile * LANES, LANES), LANES)


def each_tile(width, work, unroll=16):
    def step(tile, carry):
        work(tile, tile_at(tile))
        return carry

    tiles = width // LANES
    lax.fori_loop(0, tiles, step, 0, unroll=min(unroll, tiles))


def iota(rows, dim):
    return lax.broadcasted_iota(jnp.int32, (rows, LANES), dim)


def down(cells, by):
    return pltpu.roll(cells, by, 0)


def around(ref, index, tile, tiles, circular=True):
    cells = ref[index, :, tile_at(tile)]
    before = ref[index, :, tile_at(lax.rem(tile + tiles - 1, tiles))]
    after = ref[index, :, tile_at(lax.rem(tile + 1, tiles))]
    lane = iota(cells.shape[0], 1)
    west = pltpu.roll(jnp.where(lane == LANES - 1, before, cells), 1, 1)
    east = pltpu.roll(jnp.where(lane == 0, after, cells), LANES - 1, 1)
    return cells, west + east + (down(cells, 1) + down(cells, cells.shape[0] - 1))


def places(tm_count):
    t = lax.axis_index("tm")
    odd = lax.rem(t, 2)
    return odd, jnp.where(odd == 1, t < tm_count - 1, t > 0).astype(F32)


def lat_places(lat_count):
    l = lax.axis_index("lat")
    return lax.rem(l, 2) == 0, (l < lat_count - 1).astype(F32), (l > 0).astype(F32)


def mirrored(odd, j):
    return jnp.where(odd == 1, SLICES - 1 - j, j)


def edge_rows(blocks):
    return (2 * blocks + 7) // 8 * 8


def corner_kernel(s0, s1, s2, s3, rng, even_out, odd_out, held, even_two, odd_one, across):
    held[...] = rng[...]
    even_two[:ROWS] = s3[...]
    even_two[ROWS:] = s2[...]
    odd_one[...] = s0[...]
    chunk = rng.shape[1]
    blocks = s0.shape[1] // chunk
    for b in range(blocks):
        across[b * ROWS : (b + 1) * ROWS] = s1[:, b * chunk : (b + 1) * chunk]
    across[blocks * ROWS :] = rng[...]
    sub = iota(8, 0)
    for cells, out in ((s3, even_out), (s0, odd_out)):
        out[:ROWS] = rng[...]
        for tile in range(chunk // LANES):
            for v in range(0, edge_rows(blocks), 8):
                rows = jnp.zeros((8, LANES), F32)
                for k in range(min(4, blocks - v // 2)):
                    cols = pl.ds((v // 2 + k) * chunk + tile * LANES, LANES)
                    rows = jnp.where(sub == 2 * k, down(cells[:8, cols], 2 * k), rows)
                    rows = jnp.where(sub == 2 * k + 1, down(cells[8:, cols], (2 * k + 2) % 8), rows)
                out[ROWS + v : ROWS + v + 8, tile * LANES : (tile + 1) * LANES] = rows


def slab(ref, tile):
    per = ref.shape[1] // LANES
    at = pl.multiple_of(lax.div(tile, per) * ROWS, ROWS)
    return ref[pl.ds(at, ROWS), tile_at(lax.rem(tile, per))]


def rows_kernel(forward, *refs):
    slabs, (near_e, near_o), refs = refs[:SLICES], refs[SLICES : SLICES + 2], refs[SLICES + 2 :]
    even_lat, _, _ = lat_places(2)
    *field, full, la, lb = refs
    if forward:
        t = lax.axis_index("tm")
        chunk = field[0].shape[1]
        for i, piece in enumerate((field[0], near_e, field[1], near_o)):
            start = piece.shape[0] - ROWS if i == 2 else 0
            full[:, pl.ds(pl.multiple_of((t ^ i) * chunk, chunk), chunk)] = piece[start : start + ROWS]
    else:
        full[...] = field[0][...]
    sub = iota(8, 0)

    per = near_e.shape[1] // LANES
    for tile in range(full.shape[1] // LANES):
        cols = pl.ds(tile * LANES, LANES)
        k, at = tile // per % 4, ROWS + tile // per // 4 * 8
        for i, corner in enumerate((near_e, near_o)):
            rows = corner[at : at + 8, tile % per * LANES : (tile % per + 1) * LANES]
            one, two, field = slabs[2 * i], slabs[2 * i + 1], full
            first = jnp.where(sub == 3, down(field[:8, cols], 3 - i), down(two[:8, cols], 5))
            first = jnp.where(sub == 4, down(rows, (4 - 2 * k) % 8), first)
            first = jnp.where(sub < 3, one[:8, cols], first)
            last = jnp.where(sub == 4, down(field[8:, cols], 6 - i), down(two[8:, cols], 3))
            last = jnp.where(sub == 3, down(rows, (2 - 2 * k) % 8), last)
            last = jnp.where(sub > 4, one[8:, cols], last)
            la[8 * i : 8 * i + 8, cols] = jnp.where(even_lat, last, first)
            lb[8 * i : 8 * i + 8, cols] = jnp.where(even_lat, first, last)


def below_above(lat_count, la, lb, at, cols):
    even_lat, has_below, has_above = lat_places(lat_count)
    a, b = la[pl.ds(at, 8), cols], lb[pl.ds(at, 8), cols]
    return jnp.where(even_lat, a, b) * has_below, jnp.where(even_lat, b, a) * has_above


def joined(cells, below, above):
    return jnp.concatenate([cells, jnp.where(iota(8, 0) < 4, below, above)], axis=0)


def lat_mask(lat_count):
    _, has_below, has_above = lat_places(lat_count)
    row = iota(HELD, 0)
    return jnp.where(row < ROWS, 1.0, jnp.where(row < ROWS + 4, has_below, has_above))


def at(cells, j):
    return cells[j] if 0 <= j < SLICES else 0.0


def own_kernel(counts, s0, s1, s2, s3, full, la, lb, by0, by1, by2, grad, noise, rr, u, y1, y2, end_e, other):
    tm_count, lat_count = counts
    K0, K1, K2, _ = COEFFS
    odd, has_before = places(tm_count)
    width = full.shape[1]
    tiles = width // LANES
    mask = lat_mask(lat_count)
    back = 1.0 + has_before

    tm_four = tm_count == 4

    def gather(tile, cols):
        first, last = below_above(lat_count, la, lb, 0, cols)
        second, ahead = below_above(lat_count, la, lb, 8, cols)
        u[0, :, cols] = joined(s0[:, cols], first, last)
        u[1, :, cols] = joined(s1[:, cols], down(first, 3), down(last, 5))
        u[2, :, cols] = joined(s2[:, cols], second, ahead)
        u[3, :, cols] = joined(s3[:, cols], down(second, 3), down(ahead, 5))
        sub = iota(8, 0)
        end_e[:8, cols] = s1[:8, cols] + jnp.where(sub == 0, 3.0 * (down(ahead, 1) + down(ahead, 7)), 0.0)
        end_e[8:, cols] = s1[8:, cols] + jnp.where(sub == 7, 3.0 * (down(second, 7) + down(second, 1)), 0.0)
        if not tm_four:
            other[:8, cols] = s2[:8, cols] + jnp.where(sub == 0, 3.0 * (down(last, 6) + down(last, 2)), 0.0)
            other[8:, cols] = s2[8:, cols] + jnp.where(sub == 7, 3.0 * (down(first, 2) + down(first, 6)), 0.0)
        below = jnp.where(sub == 0, down(first, 5), down(second, 6))
        above = jnp.where(sub == 7, down(ahead, 3), down(last, 2))
        rr[:, cols] = joined(full[:, cols], below, above) + 6.0

    each_tile(width, gather)

    def once(tile, cols):
        field = rr[:, cols]
        for j in range(SLICES):
            cells, beside = around(u, j, tile, tiles)
            y1[j, :, cols] = (beside - field * cells) * mask

    each_tile(width, once)

    def twice(tile, cols):
        field = rr[:, cols]
        c0 = [u[j, :ROWS, cols] for j in range(SLICES)]
        c1 = [y1[j, :ROWS, cols] for j in range(SLICES)]
        total = jnp.zeros((ROWS, LANES), F32)
        for j in range(SLICES):
            cells, beside = around(y1, j, tile, tiles)
            c2 = (beside - field * cells) * mask
            y2[j, :, cols] = c2
            one = c1[j] + (at(c0, j - 1) + at(c0, j + 1))
            two = c2[:ROWS] + 2.0 * (at(c1, j - 1) + at(c1, j + 1))
            two = two + (back if j == 0 else 2.0) * c0[j] + (at(c0, j - 2) + at(c0, j + 2))
            place = pl.ds(mirrored(odd, j), 1)
            total = total + c0[j] * by0[place, :, cols][0] + one * by1[place, :, cols][0] + two * by2[place, :, cols][0]
            noise[j, :, cols] = K0 * c0[j] + K1 * one + K2 * two
        grad[:, cols] = -total

    each_tile(width, twice)
    if not tm_four:
        return
    chunk = other.shape[1]
    blocks = width // chunk
    sub = iota(8, 0)
    for tile in range(chunk // LANES):
        for v in range(0, edge_rows(blocks), 8):
            rows = jnp.zeros((8, LANES), F32)
            for k in range(min(4, blocks - v // 2)):
                cols = pl.ds((v // 2 + k) * chunk + tile * LANES, LANES)
                below, above = below_above(lat_count, la, lb, 0, cols)
                below = down(below, (2 * k + 4) % 8) + down(below, 2 * k)
                above = down(above, (2 * k + 6) % 8) + down(above, (2 * k + 2) % 8)
                rows = jnp.where(sub == 2 * k, above, jnp.where(sub == 2 * k + 1, below, rows))
            other[v : v + 8, tile * LANES : (tile + 1) * LANES] = rows


def near_kernel(counts, forward, grad, near_e, near_o, far_o, la, lb, rr, edge_o, by1, by2, *refs):
    tm_count, lat_count = counts
    odd, has_before = places(tm_count)
    width = grad.shape[1]
    tiles = width // LANES
    mask = lat_mask(lat_count)
    u, y1 = refs[:2]
    total = refs[-1] if forward else refs[2]
    sub = iota(8, 0)

    def gather(tile, cols):
        for i, cells in ((1, near_e), (0, near_o)):
            below, above = below_above(lat_count, la, lb, 8 - 8 * i, cols)
            edge = jnp.where(sub == 0, down(below, 4), jnp.where(sub == 7, down(above, 4), 0.0))
            cells = jnp.concatenate([cells[:ROWS, cols], edge], axis=0)
            u[i, :, cols] = cells if i else cells * has_before

    each_tile(width, gather)

    def once(tile, cols):
        field = rr[:, cols]
        out = grad[:, cols]
        for i in range(2):
            cells, beside = around(u, i, tile, tiles)
            c1 = (beside - field * cells) * mask
            y1[i, :, cols] = c1
            beyond = slab(far_o, tile) * has_before if i == 0 else near_e[ROWS:, cols]
            j, inner = (0, 1) if i == 0 else (SLICES - 1, SLICES - 2)
            j, inner = pl.ds(mirrored(odd, j), 1), pl.ds(mirrored(odd, inner), 1)
            add = cells[:ROWS] * (by1[j, :, cols][0] + by2[inner, :, cols][0])
            out = out - (add + (2.0 * c1[:ROWS] + beyond) * by2[j, :, cols][0])
        total[:, cols] = out

    each_tile(width, once)
    if forward:
        t = lax.axis_index("tm")
        chunk = refs[2].shape[1]
        for i, out in enumerate(refs[2:6]):
            out[:ROWS] = total[:, pl.ds(pl.multiple_of((t ^ i) * chunk, chunk), chunk)]
        refs[5][ROWS:] = edge_o[...]
def noise_kernel(tm_count, own, p0, p1, p2, u, y1, rr, near_e, far_o, end_e, end_o, noise, first, out, sems):
    odd, has_before = places(tm_count)
    width = own.shape[2]
    tiles = width // LANES
    _, K1, K2, K3 = COEFFS
    back = 1.0 + has_before
    row, lane = iota(ROWS, 0), iota(ROWS, 1)

    def work(tile, cols):
        field = rr[:ROWS, cols]
        c0, c1, c2 = ([ref[j, :ROWS, cols] for j in range(SLICES)] for ref in (p0, p1, p2))
        result = []
        for j in range(SLICES):
            cells, beside = around(p2, j, tile, tiles)
            three = beside[:ROWS] - field * cells[:ROWS]
            three = three + 3.0 * (at(c2, j - 1) + at(c2, j + 1) + at(c1, j - 2) + at(c1, j + 2))
            three = three + (3.0 * back if j == 0 else 6.0) * c1[j]
            left, right = (1.0 + back if j == i else 3.0 for i in (1, 0))
            three = three + (left * at(c0, j - 1) + right * at(c0, j + 1) + at(c0, j - 3) + at(c0, j + 3))
            result.append(own[j, :, cols] + K3 * three)
        for i, end in enumerate((end_o, end_e)):
            far = (lambda at: slab(far_o, at)) if i == 0 else (lambda at: near_e[ROWS:, tile_at(at)])
            cells, beside = around(y1, i, tile, tiles)
            n0, n1 = u[i, :ROWS, cols], cells[:ROWS]
            n2 = beside[:ROWS] - field * n1
            f0 = far(tile)
            before = far(lax.rem(tile + tiles - 1, tiles))
            after = far(lax.rem(tile + 1, tiles))
            west = pltpu.roll(jnp.where(lane == LANES - 1, before, f0), 1, 1)
            east = pltpu.roll(jnp.where(lane == 0, after, f0), LANES - 1, 1)
            above = jnp.where(row == 0, 0.0, down(f0, 1))
            below = jnp.where(row == ROWS - 1, 0.0, down(f0, ROWS - 1))
            f1 = west + east + (above + below) - field * f0
            beyond = 3.0 * f1 + end[:, cols]
            if i == 0:
                f0, beyond = f0 * has_before, beyond * has_before
            a, b, c = (0, 1, 2) if i == 0 else (3, 2, 1)
            result[a] = result[a] + (K1 + 3.0 * K3) * n0 + K2 * (2.0 * n1 + f0) + K3 * (3.0 * n2 + beyond)
            result[b] = result[b] + K2 * n0 + K3 * (3.0 * n1 + f0)
            result[c] = result[c] + K3 * n0
        first[:, cols] = result[0]
        for j in range(1, SLICES):
            out[j - 1, :, cols] = result[j]

    copies = []
    per = min(4, tiles)
    for q in range(0, tiles, per):

        def step(tile, carry):
            work(tile, tile_at(tile))
            return carry

        lax.fori_loop(q, q + per, step, 0, unroll=per)
        cols = pl.ds(q * LANES, per * LANES)
        for j in range(1, SLICES):
            copy = pltpu.make_async_copy(
                out.at[j - 1, :, cols],
                noise.at[mirrored(odd, j), :, cols],
                sems.at[q // per * (SLICES - 1) + j - 1],
            )
            copy.start()
            copies.append(copy)
    for copy in copies:
        copy.wait()


def last_kernel(tm_count, _, first, *refs):
    *parts, noise, gradient, out, total, sems = refs
    odd, has_before = places(tm_count)
    for i, more in enumerate(parts):
        total[...] = more[:ROWS] if i == 0 else total[...] + more[:ROWS]
    copies = [pltpu.make_async_copy(total, gradient, sems.at[0])]
    copies[0].start()
    chunk = total.shape[1]
    blocks = first.shape[1] // chunk
    scale = 3.0 * COEFFS[3] * has_before
    sub = iota(8, 0)
    if tm_count != 4:
        out[...] = first[...]
    else:
        edges = parts[-1]
        for b in range(blocks):
            for tile in range(chunk // LANES):
                k, at = b % 4, ROWS + b // 4 * 8
                rows = scale * edges[at : at + 8, tile * LANES : (tile + 1) * LANES]
                cols = pl.ds(b * chunk + tile * LANES, LANES)
                out[:8, cols] = first[:8, cols] + jnp.where(sub == 0, down(rows, (8 - 2 * k) % 8), 0.0)
                out[8:, cols] = first[8:, cols] + jnp.where(sub == 7, down(rows, 6 - 2 * k), 0.0)
    copies.append(pltpu.make_async_copy(out, noise.at[mirrored(odd, 0)], sems.at[1]))
    copies[1].start()
    for copy in copies:
        copy.wait()


def body(counts, cotangent, iterates, range_field):
    tm_count, lat_count = counts
    forward = tm_count == 4
    slices, rows, width = cotangent.shape
    chunk = range_field.shape[1]
    assert slices == SLICES and rows == ROWS
    even, odd = even_pairs(tm_count), odd_pairs(tm_count)
    lat_even, lat_odd = even_pairs(lat_count), lat_odd_pairs(tm_count, lat_count)
    inner = inner_odd_pairs(tm_count, lat_count)
    y_pairs = [(i, i ^ 2) for i in range(tm_count)]
    one = shape_of(ROWS, width)
    extra = edge_rows(width // chunk)

    flip = lax.rem(lax.axis_index("tm"), 2) == 1
    slabs = [
        lax.dynamic_index_in_dim(cotangent, jnp.where(flip, SLICES - 1 - j, j), 0, False) for j in range(SLICES)
    ]
    message = shape_of(ROWS + edge_rows(width // chunk), chunk)
    two = shape_of(2 * ROWS, width)
    corner_e, corner_o, held, near_e, near_o, across = call(
        corner_kernel, [message, message, shape_of(ROWS, chunk), two, one, shape_of(width // chunk * ROWS + ROWS, chunk)], *slabs, range_field
    )
    corner_e, corner_o = lax.ppermute(corner_e, "tm", even), lax.ppermute(corner_o, "tm", odd)
    if forward:
        across = lax.ppermute(across, "tm", y_pairs)
        field = [held, across]
        far_o = lax.ppermute(across[: width // chunk * ROWS], "tm", [(0, 1), (1, 3), (3, 2), (2, 0)])
    else:
        field = [lax.all_gather(range_field, "tm", axis=1, tiled=True)]
        far_o = lax.ppermute(across[: width // chunk * ROWS], ("tm", "lat"), inner)
    near_e, near_o = lax.ppermute(near_e, "tm", even), lax.ppermute(near_o, ("tm", "lat"), inner)
    x1, x2, x3 = iterates[0], iterates[1], iterates[2]
    scales = (W3 * x3 + W2 * x2 + W1 * x1, (W2 * W3) * x2 + (W1 * SUM2) * x1, (W1 * PROD2) * x1)
    pair = shape_of(16, width)
    full, la1, lb1 = call(functools.partial(rows_kernel, forward), [one, pair, pair], *slabs, corner_e, corner_o, *field)
    la1, lb1 = lax.ppermute(la1, "lat", lat_even), lax.ppermute(lb1, ("tm", "lat"), lat_odd)
    deep = shape_of(SLICES, HELD, width)
    own = shape_of(SLICES, ROWS, width)
    grad, own, rr, *powers, end_e, other = call(
        functools.partial(own_kernel, counts),
        [one, own, shape_of(HELD, width), deep, deep, deep, one, shape_of(extra, chunk) if forward else one],
        *slabs,
        full,
        la1,
        lb1,
        *scales,
    )
    end_e = lax.ppermute(end_e, "tm", even)
    if forward:
        end_o = lax.ppermute(near_e[ROWS:], "tm", y_pairs)
    else:
        end_o = lax.ppermute(other, ("tm", "lat"), inner)
    pair = shape_of(2, HELD, width)
    if forward:
        outs = [shape_of(ROWS + more, chunk) for more in (0, 0, 0, extra)]
    else:
        outs = [one]
    u, y1, *outs = call(
        functools.partial(near_kernel, counts, forward),
        [pair, pair] + outs,
        grad,
        near_e,
        near_o,
        far_o,
        la1,
        lb1,
        rr,
        other,
        *scales[1:],
        scratch=[pltpu.VMEM((ROWS, width), F32)] if forward else (),
    )
    if forward:
        parts = outs[0], *(lax.ppermute(g, "tm", p) for g, p in zip(outs[1:], (even, y_pairs, odd)))
    else:
        parts = (lax.psum_scatter(outs[0], "tm", scatter_dimension=1, tiled=True),)
    quarters = width // LANES // min(4, width // LANES)
    noise, first = call(
        functools.partial(noise_kernel, tm_count),
        [shape_of(SLICES, ROWS, width), one],
        own,
        *powers,
        u,
        y1,
        rr,
        near_e,
        far_o,
        end_e,
        end_o,
        out_specs=[ANYWHERE, IN_PLACE],
        scratch=[
            pltpu.VMEM((SLICES - 1, ROWS, width), F32),
            pltpu.SemaphoreType.DMA((quarters * (SLICES - 1),)),
        ],
    )
    return call(
        functools.partial(last_kernel, tm_count),
        [shape_of(SLICES, ROWS, width), shape_of(ROWS, chunk)],
        noise,
        first,
        *parts,
        in_specs=[ANYWHERE] + [IN_PLACE] * (1 + len(parts)),
        out_specs=[ANYWHERE, ANYWHERE],
        scratch=[pltpu.VMEM((ROWS, width), F32), pltpu.VMEM((ROWS, chunk), F32), pltpu.SemaphoreType.DMA((2,))],
        aliases={0: 0},
    )


def solution(mesh):
    counts = (mesh.shape["tm"], mesh.shape["lat"])
    return jax.shard_map(
        functools.partial(body, counts),
        mesh=mesh,
        in_specs=(P("tm", "lat", None), P(None, "tm", "lat", None), P("lat", "tm")),
        out_specs=(P("tm", "lat", None), P("lat", "tm")),
        check_vma=False,
    )
```
